32 devices in a mesh: store: 4 (over z), scorer: 8 (over y, x, core).
Axes of the slice: x: 2, y: 2, z: 4, core: 2. Of those that a mesh axis runs over, the one named last changes fastest.
Arguments:
- store_rows: bfloat16 [65536, 256], P(('store', 'scorer')), may hold values from -11 to 11
- cluster_logsize: bfloat16 [65536], P(('store', 'scorer')), may hold values from 0 to 318
- cluster_home: int32 [65536], replicated, may hold values from 0 to 65535, as said below
- cluster_ids: int32 [256, 512], P(('store', 'scorer')), may hold values from 0 to 65535, as said below
- valid_count: int32 [256], P(('store', 'scorer')), may hold values from 64 to 512
- candidates: bfloat16 [256, 512, 256], P(('store', 'scorer')), may hold values from -11 to 11
- cand_count: int32 [256], P(('store', 'scorer')), may hold values from 0 to 512, as said below
- candidate_row: int32 [256, 512], P(('store', 'scorer')), may hold values from 0 to 16383, as said below
- query_proj: bfloat16 [256, 256], replicated, may hold values from -0.375 to 0.375
- key_proj: bfloat16 [256, 256], replicated, may hold values from -0.375 to 0.375
- value_proj: bfloat16 [256, 256], replicated, may hold values from -0.375 to 0.375
- out_proj: bfloat16 [256, 256], replicated, may hold values from -0.375 to 0.375
- mlp_first: bfloat16 [512, 512], replicated, may hold values from -0.25 to 0.25
- bias_first: float32 [512], replicated, may hold values from -3 to 3
- mlp_second: bfloat16 [512, 256], replicated, may hold values from -0.25 to 0.25
- bias_second: float32 [256], replicated, may hold values from -3 to 3
- score_proj: bfloat16 [256], replicated, may hold values from -0.375 to 0.375
Outputs:
- span_scores: float32 [65536], P(('store', 'scorer'))
The draws below stay inside these ranges and needn't reach their ends.
Inputs may be any that keep to these rules, and one draw needn't show every extreme that they name: A permutation: cluster c is row cluster_home[c] of store_rows. `cluster_ids`: of the 4096 entries of one device's requests, exactly 128 name clusters whose rows lie on each device's rows of store_rows, valid slots or not. `cand_count`: the counts of the 8 devices of one store group sum to 16384; in every group one device has all its requests full. `candidate_row`: the valid candidates of a store group fill each of its 16384 rows once; rows c * 2048 to (c + 1) * 2048 - 1 form span c, held by the group's device of scorer index c. One device has at most 512 valid candidates in one span, and in every group one device has exactly 512 in each span. Padded slots hold 0.
All inputs are finite; a program needn't handle non-finite values.
Results may differ from the reference program's by a relative error of at most 0.0065.
Values may be sent and summed in bfloat16 or wider, within the bound.
No kernel may reach another device: no remote copies, remote signals or barrier semaphores. Data moves between devices by JAX's collectives and lax.ppermute only.
A program may use at most 128 MiB of HBM per device.

```python
import math
import jax
import jax.numpy as jnp
from jax import lax

W = 256
HEADS = 4
K = 512
M1 = 512
M2 = 256
REQ_DEV = 8
CAND_CAP = 512
ROWS_DEV = 2048
REQS = 256
CLUSTERS = 65536
SPAN_LIVE = 2048
SCORE_ROWS = 65536
N_SCORER = 8


def placing(key):
    return jax.random.permutation(jax.random.fold_in(key, 101), CLUSTERS).astype(jnp.int32)


def shared_direction(key):
    return jnp.clip(jax.random.normal(jax.random.fold_in(key, 404), (W,), jnp.float32), -3.0, 3.0)


def listed_clusters(key):
    shared = placing(key)
    key = jax.random.fold_in(key, 303)
    device_count = REQS // REQ_DEV
    slot_total = REQ_DEV * K
    subkeys = jax.random.split(key, device_count + 1)
    shuffles = jax.vmap(lambda subkey: jax.random.permutation(subkey, slot_total))(subkeys[:device_count])
    home_dev = (shuffles % device_count).astype(jnp.int32)
    local_row = jax.random.randint(subkeys[device_count], (device_count, slot_total), 0, ROWS_DEV, dtype=jnp.int32)
    cluster_at = jnp.zeros((CLUSTERS,), jnp.int32).at[shared].set(jnp.arange(CLUSTERS, dtype=jnp.int32))
    return cluster_at[home_dev * ROWS_DEV + local_row].reshape(REQS, K)


def candidate_plan(key):
    key = jax.random.fold_in(key, 202)
    subkeys = jax.random.split(key, 5)
    groups = REQS // (REQ_DEV * N_SCORER)
    halves = N_SCORER // 2
    own_max = REQ_DEV * CAND_CAP
    span_live = own_max // 2
    amounts = jax.random.randint(subkeys[0], (groups, halves), 0, own_max + 1, dtype=jnp.int32)
    forced = jax.random.randint(subkeys[1], (groups, 1), 0, halves, dtype=jnp.int32)
    amounts = jnp.where(jnp.arange(halves, dtype=jnp.int32)[None, :] == forced, own_max, amounts)
    totals = jnp.concatenate([amounts, own_max - amounts], axis=1)
    owner_order = jax.vmap(lambda subkey: jax.random.permutation(subkey, N_SCORER))(jax.random.split(subkeys[2], groups))
    totals = jnp.take_along_axis(totals, owner_order.astype(jnp.int32), axis=1)
    filled = jnp.clip(totals[:, :, None] - CAND_CAP * jnp.arange(REQ_DEV, dtype=jnp.int32)[None, None, :], 0, CAND_CAP)
    request_order = jax.vmap(lambda subkey: jax.random.permutation(subkey, REQ_DEV))(jax.random.split(subkeys[3], groups * N_SCORER))
    request_order = request_order.reshape(groups, N_SCORER, REQ_DEV).astype(jnp.int32)
    counts = jnp.take_along_axis(filled, request_order, axis=2).astype(jnp.int32)
    flat = counts.reshape(groups, N_SCORER * REQ_DEV)
    offsets = jnp.cumsum(flat, axis=1) - flat
    slot_index = jnp.arange(CAND_CAP, dtype=jnp.int32)
    serial = offsets[:, :, None] + slot_index[None, None, :]
    valid_mask = slot_index[None, None, :] < flat[:, :, None]
    span_index = serial % N_SCORER
    within = jnp.where(valid_mask, serial // N_SCORER, 0)
    shuffles = jax.vmap(lambda subkey: jax.random.permutation(subkey, span_live))(jax.random.split(subkeys[4], groups * N_SCORER))
    shuffles = shuffles.reshape(groups, N_SCORER * span_live).astype(jnp.int32)
    lookup_at = (span_index * span_live + within).reshape(groups, -1)
    picked = jnp.take_along_axis(shuffles, lookup_at, axis=1).reshape(serial.shape)
    rows_out = jnp.where(valid_mask, span_index * span_live + picked, 0).astype(jnp.int32)
    return (counts.reshape(REQS), rows_out.reshape(REQS, CAND_CAP))


def draw_store_rows(key, part):
    direction = shared_direction(key)
    key = jax.random.fold_in(key, 7)
    sign_key, noise_key = jax.random.split(key)
    signs = jnp.where(jax.random.bernoulli(sign_key, 0.5, (CLUSTERS, 1)), 1.0, -1.0).astype(jnp.float32)
    noise = jnp.clip(jax.random.normal(noise_key, (CLUSTERS, W), jnp.float32), -6.0, 6.0)
    amplitude = 1.5
    return jnp.clip(noise + amplitude * signs * direction[None, :], -11.0, 11.0).astype(jnp.bfloat16)


def draw_candidates(key, part):
    direction = shared_direction(key)
    key = jax.random.fold_in(key, 8)
    sign_key, noise_key = jax.random.split(key)
    signs = jnp.where(jax.random.bernoulli(sign_key, 0.5, (REQS, CAND_CAP, 1)), 1.0, -1.0).astype(jnp.float32)
    noise = jnp.clip(jax.random.normal(noise_key, (REQS, CAND_CAP, W), jnp.float32), -6.0, 6.0)
    amplitude = 1.5
    return jnp.clip(noise + amplitude * signs * direction[None, None, :], -11.0, 11.0).astype(jnp.bfloat16)


def draw_cluster_logsize(key, part):
    key = jax.random.fold_in(key, 6)
    return jax.random.uniform(key, (CLUSTERS,), jnp.float32, 1.6, 2.8).astype(jnp.bfloat16)


def draw_cluster_home(key, part):
    shared = placing(key)
    return shared


def draw_cluster_ids(key, part):
    listed = listed_clusters(key)
    return listed


def draw_valid_count(key, part):
    key = jax.random.fold_in(key, 3)
    first_key, second_key = jax.random.split(key)
    counts = jax.random.randint(first_key, (REQS,), K // 8, K + 1, dtype=jnp.int32)
    chosen = jax.random.randint(second_key, (), 0, REQS, dtype=jnp.int32)
    return jnp.where(jnp.arange(REQS, dtype=jnp.int32) == chosen, K, counts).astype(jnp.int32)


def draw_cand_count(key, part):
    counts, rows_out = candidate_plan(key)
    return counts


def draw_candidate_row(key, part):
    counts, rows_out = candidate_plan(key)
    return rows_out


def gaussian(stream_key, shape, scale, most, kind=jnp.bfloat16):
    result = scale * jax.random.normal(stream_key, shape, jnp.float32)
    return jnp.clip(result, min=-most, max=most).astype(kind)


def setup_inputs(seed: int = 0) -> dict:
    arg_keys = jax.random.split(jax.random.key(seed), 18)
    store_rows = draw_store_rows(jax.random.fold_in(arg_keys[17], 71), 0)
    cluster_logsize = draw_cluster_logsize(jax.random.fold_in(arg_keys[17], 71), 0)
    cluster_home = draw_cluster_home(jax.random.fold_in(arg_keys[17], 71), 0)
    cluster_ids = draw_cluster_ids(jax.random.fold_in(arg_keys[17], 71), 0)
    valid_count = draw_valid_count(jax.random.fold_in(arg_keys[17], 71), 0)
    candidates = draw_candidates(jax.random.fold_in(arg_keys[17], 71), 0)
    cand_count = draw_cand_count(jax.random.fold_in(arg_keys[17], 71), 0)
    candidate_row = draw_candidate_row(jax.random.fold_in(arg_keys[17], 71), 0)
    query_proj = gaussian(arg_keys[8], (W, W), W ** -0.5, 0.375)
    key_proj = gaussian(arg_keys[9], (W, W), W ** -0.5, 0.375)
    value_proj = gaussian(arg_keys[10], (W, W), W ** -0.5, 0.375)
    out_proj = gaussian(arg_keys[11], (W, W), W ** -0.5, 0.375)
    mlp_first = gaussian(arg_keys[12], (2 * W, M1), (2 * W) ** -0.5, 0.25)
    bias_first = gaussian(arg_keys[13], (M1,), 0.5, 3.0, jnp.float32)
    mlp_second = gaussian(arg_keys[14], (M1, M2), M1 ** -0.5, 0.25)
    bias_second = gaussian(arg_keys[15], (M2,), 0.5, 3.0, jnp.float32)
    score_proj = gaussian(arg_keys[16], (M2,), M2 ** -0.5, 0.375)
    return dict(store_rows=store_rows, cluster_logsize=cluster_logsize, cluster_home=cluster_home, cluster_ids=cluster_ids, valid_count=valid_count, candidates=candidates, cand_count=cand_count, candidate_row=candidate_row, query_proj=query_proj, key_proj=key_proj, value_proj=value_proj, out_proj=out_proj, mlp_first=mlp_first, bias_first=bias_first, mlp_second=mlp_second, bias_second=bias_second, score_proj=score_proj)


def attend(cand_block, key_rows, key_sizes, key_count, query_proj, key_proj, value_proj, out_proj):
    batch_size, cand_slots, row_width = cand_block.shape
    cluster_slots = key_rows.shape[1]
    head_size = row_width // HEADS
    queries = jnp.dot(cand_block.reshape(-1, row_width), query_proj, preferred_element_type=jnp.float32).astype(jnp.bfloat16)
    keys_all = jnp.dot(key_rows.reshape(-1, row_width), key_proj, preferred_element_type=jnp.float32).astype(jnp.bfloat16)
    values_all = jnp.dot(key_rows.reshape(-1, row_width), value_proj, preferred_element_type=jnp.float32).astype(jnp.bfloat16)
    queries = queries.reshape(batch_size, cand_slots, HEADS, head_size).astype(jnp.float32)
    keys_all = keys_all.reshape(batch_size, cluster_slots, HEADS, head_size).astype(jnp.float32)
    values_all = values_all.reshape(batch_size, cluster_slots, HEADS, head_size).astype(jnp.float32)
    logits = jnp.einsum('bchd,bkhd->bhck', queries, keys_all)
    logits = logits * (1.0 / math.sqrt(head_size)) + key_sizes.astype(jnp.float32)[:, None, None, :]
    usable = jnp.arange(cluster_slots, dtype=jnp.int32)[None, :] < key_count[:, None]
    logits = jnp.where(usable[:, None, None, :], logits, -1e+30)
    row_max = lax.optimization_barrier(jnp.max(logits, axis=-1, keepdims=True))
    weights = jnp.exp(logits - row_max)
    probs = (weights / lax.optimization_barrier(jnp.sum(weights, axis=-1, keepdims=True))).astype(jnp.bfloat16)
    context = jnp.einsum('bhck,bkhd->bchd', probs.astype(jnp.float32), values_all).astype(jnp.bfloat16)
    context = context.reshape(batch_size * cand_slots, row_width)
    attended = jnp.dot(context, out_proj, preferred_element_type=jnp.float32).astype(jnp.bfloat16)
    return attended.reshape(batch_size, cand_slots, row_width)

def score_rows(features, mlp_first, bias_first, mlp_second, bias_second, score_proj):
    hidden_one = jnp.maximum(jnp.dot(features, mlp_first, preferred_element_type=jnp.float32) + bias_first, 0.0).astype(jnp.bfloat16)
    hidden_two = jnp.maximum(jnp.dot(hidden_one, mlp_second, preferred_element_type=jnp.float32) + bias_second, 0.0).astype(jnp.bfloat16)
    return jnp.dot(hidden_two, score_proj, preferred_element_type=jnp.float32)

def reference(store_rows, cluster_logsize, cluster_home, cluster_ids, valid_count, candidates, cand_count, candidate_row, query_proj, key_proj, value_proj, out_proj, mlp_first, bias_first, mlp_second, bias_second, score_proj):
    block_total = REQS // REQ_DEV

    def one_block(block_index):
        block_start = block_index * REQ_DEV
        block_ids = lax.dynamic_slice_in_dim(cluster_ids, block_start, REQ_DEV, 0)
        global_row = cluster_home[block_ids]
        block_rows = store_rows[global_row]
        block_sizes = cluster_logsize[global_row]
        key_count = lax.dynamic_slice_in_dim(valid_count, block_start, REQ_DEV, 0)
        cand_block = lax.dynamic_slice_in_dim(candidates, block_start, REQ_DEV, 0)
        attended = attend(cand_block, block_rows, block_sizes, key_count, query_proj, key_proj, value_proj, out_proj)
        features = jnp.concatenate([cand_block, attended], axis=-1).reshape(REQ_DEV * CAND_CAP, 2 * W)
        return score_rows(features, mlp_first, bias_first, mlp_second, bias_second, score_proj).reshape(REQ_DEV, CAND_CAP)
    cand_score = lax.map(one_block, jnp.arange(block_total, dtype=jnp.int32)).reshape(REQS, CAND_CAP)
    group_of = jnp.arange(REQS, dtype=jnp.int32) // (REQ_DEV * N_SCORER)
    valid_mask = jnp.arange(CAND_CAP, dtype=jnp.int32)[None, :] < cand_count[:, None]
    out_index = jnp.where(valid_mask, group_of[:, None] * (N_SCORER * SPAN_LIVE) + candidate_row, SCORE_ROWS).astype(jnp.int32)
    span_scores = jnp.zeros((SCORE_ROWS,), jnp.float32).at[out_index.reshape(-1)].set(cand_score.reshape(-1), mode='drop')
    return span_scores
```

```python
import functools
import math

import jax
import jax.numpy as jnp
from jax import lax
from jax.experimental import pallas as pl
from jax.experimental.pallas import tpu as pltpu
from jax.sharding import PartitionSpec as P

HEADS = 4
LANES = 128
BLOCK = 16
DEAD = -1e30
HIGH = 65536
VMEM_LIMIT = 40 * 1024 * 1024


def dot(a, b):
    return jnp.dot(a, b, preferred_element_type=jnp.float32)


def dot_nt(a, b):
    return lax.dot_general(a, b, (((1,), (1,)), ((), ())), preferred_element_type=jnp.float32)


def hot(mask):
    return jnp.where(mask, 1.0, 0.0).astype(jnp.bfloat16)


def iota(shape, axis):
    return lax.broadcasted_iota(jnp.int32, shape, axis)


def whole(memory_space=pltpu.VMEM):
    return pl.BlockSpec(memory_space=memory_space)


def look_up(table_t, index, pieces):
    highs = table_t.shape[1]
    count = index.shape[1]
    rows = dot(table_t, hot(iota((highs, count), 0) == (index >> 7)))
    mine = iota((LANES, count), 0) == (index & (LANES - 1))
    found = jnp.zeros((1, count), jnp.float32)
    for piece in range(pieces):
        part = rows[piece * LANES : (piece + 1) * LANES]
        found = found + float(256**piece) * jnp.sum(
            jnp.where(mine, part, 0.0), axis=0, keepdims=True
        )
    return found


def ask_kernel(
    valid_ref, count_ref, ids_ref, home_ref, asked_ref, rank_ref, span_ref, table_ref, *, rows_dev
):
    requests, slots = ids_ref.shape
    devices, per_pair = asked_ref.shape
    pieces = table_ref.shape[0] // LANES
    for piece in range(pieces):
        part = (home_ref[...] >> (8 * piece)) & 255
        table_ref[piece * LANES : (piece + 1) * LANES, :] = jnp.transpose(
            part.astype(jnp.float32)
        ).astype(jnp.bfloat16)
    table = table_ref[...]
    upto = hot(iota((slots, slots), 0) <= iota((slots, slots), 1))
    carry = jnp.zeros((devices, 1), jnp.float32)
    asked = jnp.zeros((devices, 2 * per_pair), jnp.float32)
    for r in range(requests):
        row = look_up(table, ids_ref[r : r + 1, :], pieces).astype(jnp.int32)
        dev = row // rows_dev
        local = row - dev * rows_dev
        live = iota((1, slots), 1) < jnp.where(count_ref[r] > 0, valid_ref[r], 0)
        dest = jnp.where((iota((devices, slots), 0) == dev) & live, 1.0, 0.0)
        running = dot(dest.astype(jnp.bfloat16), upto) + carry
        carry = running[:, slots - 1 : slots]
        rank_f = jnp.sum(dest * running, axis=0, keepdims=True) - 1.0
        rank = rank_f.astype(jnp.int32)
        at_rank = iota((per_pair, slots), 0) == rank
        local_f = local.astype(jnp.float32)
        high_f = (local >> 8).astype(jnp.float32)
        low_f = local_f - 256.0 * high_f
        values = jnp.concatenate(
            [jnp.where(at_rank, low_f, 0.0), jnp.where(at_rank, high_f, 0.0)], axis=0
        )
        asked = asked + dot_nt(dest.astype(jnp.bfloat16), values.astype(jnp.bfloat16))
        rank_ref[r : r + 1, :] = jnp.where(live, dev * LANES + rank, -1)
        span_ref[r] = jnp.min(jnp.where(live, rank_f, 1e9)).astype(jnp.int32)
        span_ref[requests + r] = jnp.max(rank_f).astype(jnp.int32)
    most = jnp.max(carry, axis=0, keepdims=True)
    asked = asked[:, :per_pair] + 256.0 * asked[:, per_pair:] + HIGH * most
    asked_ref[...] = asked.astype(jnp.int32)


def ask(valid_count, cand_count, cluster_ids, home_table, devices, per_pair, rows_dev):
    requests, slots = cluster_ids.shape
    highs = home_table.shape[0]
    pieces = -(-(highs * LANES - 1).bit_length() // 8)
    return pl.pallas_call(
        functools.partial(ask_kernel, rows_dev=rows_dev),
        in_specs=[whole(pltpu.SMEM), whole(pltpu.SMEM), whole(), whole()],
        out_specs=[whole(), whole(), whole(pltpu.SMEM)],
        out_shape=[
            jax.ShapeDtypeStruct((devices, per_pair), jnp.int32),
            jax.ShapeDtypeStruct((requests, slots), jnp.int32),
            jax.ShapeDtypeStruct((2 * requests,), jnp.int32),
        ],
        scratch_shapes=[pltpu.VMEM((pieces * LANES, highs), jnp.bfloat16)],
        compiler_params=pltpu.CompilerParams(vmem_limit_bytes=VMEM_LIMIT),
        cost_estimate=pl.CostEstimate(
            flops=4_000_000_000, bytes_accessed=1_000_000, transcendentals=0
        ),
        name="ask",
    )(valid_count, cand_count, cluster_ids, home_table)


def serve_kernel(asked_ref, store_ref, size_ref, *refs, first, sized):
    out_refs, column_ref = refs[:-1], refs[-1]
    devices, per_pair = asked_ref.shape
    rows_dev, width = store_ref.shape
    places = max(out_ref.shape[1] for out_ref in out_refs)
    asked = asked_ref[...] & (HIGH - 1)
    column_ref[...] = jnp.zeros(column_ref.shape, jnp.int32)
    column_ref[1 : per_pair + 1, :] = jnp.transpose(asked.astype(jnp.float32)).astype(jnp.int32)
    group = math.gcd(devices, 1 << (384 // places).bit_length() - 1)
    store = store_ref[...]
    lanes = iota((places, rows_dev), 1)
    if sized:
        size_t = jnp.transpose(size_ref[...].astype(jnp.float32)).astype(jnp.bfloat16)
    for start in range(0, devices, group):
        picks = []
        for d in range(start, start + group):
            column = column_ref[first : first + places, d : d + 1]
            picks.append(hot(column == lanes))
        found = dot(jnp.concatenate(picks, axis=0), store).reshape(group, places, width)
        if sized:
            asked_of = [asked[d : d + 1, :] for d in range(start, start + group)]
            sizes = look_up(size_t, jnp.concatenate(asked_of, axis=1), 1)
            rest = jnp.zeros((1, width - per_pair), jnp.float32)
            for g in range(group):
                mine = sizes[:, g * per_pair : (g + 1) * per_pair]
                mine = jnp.concatenate([mine, rest], axis=1)
                top = jnp.where(iota((places, width), 0) == 0, mine, found[g])
                out_refs[0][start + g] = top.astype(jnp.bfloat16)
        else:
            found = found.astype(jnp.bfloat16)
            for out_ref in out_refs:
                out_ref[start : start + group] = found[:, : out_ref.shape[1], :]


def serve(asked_here, store_rows, size_table, first, place_counts, sized):
    devices, per_pair = asked_here.shape
    rows_dev, width = store_rows.shape
    places = max(place_counts)
    column_rows = max(first + places, -(-(per_pair + 1) // BLOCK) * BLOCK)
    return pl.pallas_call(
        functools.partial(serve_kernel, first=first, sized=sized),
        in_specs=[whole(), whole(), whole()],
        out_specs=[whole() for _ in place_counts],
        out_shape=[
            jax.ShapeDtypeStruct((devices, count, width), jnp.bfloat16) for count in place_counts
        ],
        scratch_shapes=[pltpu.VMEM((column_rows, devices), jnp.int32)],
        compiler_params=pltpu.CompilerParams(vmem_limit_bytes=VMEM_LIMIT),
        cost_estimate=pl.CostEstimate(
            flops=2 * devices * places * rows_dev * width,
            bytes_accessed=2 * (rows_dev + devices * sum(place_counts)) * width,
            transcendentals=0,
        ),
        name="serve",
    )(asked_here, store_rows, size_table)


def column_of(row):
    return jnp.transpose(jnp.broadcast_to(row, (LANES, row.shape[1])))


def score_kernel(*refs, bases, from_place, to_place):
    (valid_ref, count_ref, span_ref, cand_ref, rank_ref, target_ref) = refs[:6]
    arrived_refs = refs[6 : 6 + len(bases)]
    (
        query_ref,
        key_ref,
        value_ref,
        out_proj_ref,
        first_ref,
        bias_first_ref,
        second_ref,
        bias_second_ref,
        score_ref,
        before_ref,
        table_ref,
        rows_ref,
        keys_ref,
        values_ref,
        size_ref,
    ) = refs[6 + len(bases) :]
    requests, slots = rank_ref.shape
    devices = arrived_refs[0].shape[0]
    cands, width = cand_ref.shape[1:]
    head_size = width // HEADS
    r = pl.program_id(0)
    valid = valid_ref[r]
    count = count_ref[r]
    first_place = span_ref[r] + 1
    last_place = span_ref[requests + r] + 1
    low_block = first_place // BLOCK
    high_block = last_place // BLOCK
    mine = (count > 0) & (last_place >= from_place) & (last_place < to_place)
    cand_part = math.gcd(cands, 256)
    highs = table_ref.shape[0]
    to_exp2 = math.log2(math.e) / math.sqrt(head_size)

    @pl.when(r == 0)
    def _():
        table_ref[...] = before_ref[...]
        heads_of = arrived_refs[0][:, :BLOCK, :LANES].astype(jnp.float32)
        at_top = iota(heads_of.shape, 1) == 0
        sizes = jnp.sum(jnp.where(at_top, heads_of, 0.0), axis=1)
        size_ref[...] = jnp.transpose(sizes).astype(jnp.bfloat16)

    def run(n):
        spot = rank_ref[pl.ds(r, 1), :n]
        at = (spot & (LANES - 1)) + 1
        place = (at // BLOCK) * (devices * BLOCK) + (spot // LANES) * BLOCK + at % BLOCK
        place = column_of(jnp.where(spot >= 0, place, -1))
        offset = look_up(size_ref[...], spot, 1) * math.sqrt(head_size)
        offset = jnp.where(spot >= 0, offset, DEAD)
        rows_ref[:n, :] = jnp.zeros((n, width), jnp.float32)
        for arrived_ref, base in zip(arrived_refs, bases):
            block_rows = devices * BLOCK
            blocks = arrived_ref.shape[1] // BLOCK

            def add_block(j, carry):
                start = pl.multiple_of(j * BLOCK, BLOCK)
                block = arrived_ref[:, pl.ds(start, BLOCK), :].reshape(block_rows, width)
                rel = place - (j + base) * block_rows
                lanes = iota((n, LANES), 1)
                picks = [hot(rel == lanes + g * LANES) for g in range(block_rows // LANES)]
                rows_ref[:n, :] += dot(jnp.concatenate(picks, axis=1), block)
                return carry

            lax.fori_loop(
                jnp.clip(low_block - base, 0, blocks),
                jnp.clip(high_block + 1 - base, 0, blocks),
                add_block,
                0,
            )
        rows = rows_ref[:n, :].astype(jnp.bfloat16)
        keys = dot(rows, key_ref[...]).astype(jnp.bfloat16)
        values = dot(rows, value_ref[...]).astype(jnp.bfloat16)
        head_of = iota((n, width), 1) // head_size
        zero = jnp.zeros((n, width), jnp.bfloat16)
        for h in range(HEADS):
            keys_ref[h, :n, :] = jnp.where(head_of == h, keys, zero)
            values_ref[h, :n, :] = jnp.where(head_of == h, values, zero)

        def part(c, carry):
            start = pl.multiple_of(c * cand_part, cand_part)
            cand = cand_ref[0, pl.ds(start, cand_part), :]
            queries = dot(cand, query_ref[...]).astype(jnp.bfloat16)
            context = jnp.zeros((cand_part, width), jnp.float32)
            for h in range(HEADS):
                logits = dot_nt(queries, keys_ref[h, :n, :]) + offset
                top = jnp.max(logits, axis=1, keepdims=True)
                weights = jnp.exp2((logits - top) * to_exp2)
                probs = weights * (1.0 / jnp.sum(weights, axis=1, keepdims=True))
                context = context + dot(probs.astype(jnp.bfloat16), values_ref[h, :n, :])
            attended = dot(context.astype(jnp.bfloat16), out_proj_ref[...]).astype(jnp.bfloat16)
            hidden = (
                dot(cand, first_ref[:width, :])
                + dot(attended, first_ref[width:, :])
                + bias_first_ref[...]
            )
            hidden = jnp.maximum(hidden, 0.0).astype(jnp.bfloat16)
            hidden = dot(hidden, second_ref[...]) + bias_second_ref[...]
            hidden = jnp.maximum(hidden, 0.0).astype(jnp.bfloat16)
            scores = dot_nt(jnp.broadcast_to(score_ref[...], (8, hidden.shape[1])), hidden)[:1]
            target = target_ref[pl.ds(r, 1), pl.ds(start, cand_part)]
            counted = iota((1, cand_part), 1) + start < count
            high_hot = hot((iota((highs, cand_part), 0) == (target >> 7)) & counted)
            at_low = iota((LANES, cand_part), 0) == (target & (LANES - 1))
            left = scores
            for _ in range(3):
                piece = left.astype(jnp.bfloat16).astype(jnp.float32)
                left = left - piece
                table_ref[...] += dot_nt(
                    high_hot, jnp.where(at_low, piece, 0.0).astype(jnp.bfloat16)
                )
            return carry

        lax.fori_loop(0, (count + cand_part - 1) // cand_part, part, 0)

    step = max(LANES, slots // 2)
    for n in range(step, slots + 1, step):

        @pl.when(mine & (valid > n - step) & (valid <= n))
        def _():
            run(n)


def score(scalars, candidates, ranks, candidate_row, arrived, weights, before, places):
    requests, cands, width = candidates.shape
    slots = ranks.shape[1]
    devices = arrived[0].shape[0]
    full = lambda shape: pl.BlockSpec(shape, lambda r, *_: (0,) * len(shape))
    highs = before.shape[0]
    bases = (0, arrived[0].shape[1] // BLOCK)[: len(arrived)]
    operands = [ranks, candidate_row, *arrived, *weights, before]
    return pl.pallas_call(
        functools.partial(score_kernel, bases=bases, from_place=places[0], to_place=places[1]),
        grid_spec=pltpu.PrefetchScalarGridSpec(
            num_scalar_prefetch=3,
            grid=(requests,),
            in_specs=[pl.BlockSpec((1, cands, width), lambda r, *_: (r, 0, 0))]
            + [full(x.shape) for x in operands],
            out_specs=full((highs, LANES)),
            scratch_shapes=[
                pltpu.VMEM((slots, width), jnp.float32),
                pltpu.VMEM((HEADS, slots, width), jnp.bfloat16),
                pltpu.VMEM((HEADS, slots, width), jnp.bfloat16),
                pltpu.VMEM((LANES, devices), jnp.bfloat16),
            ],
        ),
        out_shape=jax.ShapeDtypeStruct((highs, LANES), jnp.float32),
        compiler_params=pltpu.CompilerParams(
            vmem_limit_bytes=VMEM_LIMIT, dimension_semantics=("arbitrary",)
        ),
        cost_estimate=pl.CostEstimate(
            flops=10_000_000_000, bytes_accessed=5_000_000, transcendentals=4_000_000
        ),
        name="score",
    )(*scalars, candidates, *operands)


def on_device(
    store_rows,
    cluster_logsize,
    cluster_home,
    cluster_ids,
    valid_count,
    candidates,
    cand_count,
    candidate_row,
    query_proj,
    key_proj,
    value_proj,
    out_proj,
    mlp_first,
    bias_first,
    mlp_second,
    bias_second,
    score_proj,
):
    axes = ("store", "scorer")
    devices = lax.axis_size(axes)
    scorers = lax.axis_size("scorer")
    requests, slots = cluster_ids.shape
    rows_dev, width = store_rows.shape
    cands = candidates.shape[1]
    per_pair = requests * slots // devices
    span_live = requests * cands // 2

    exchange = functools.partial(
        lax.all_to_all, axis_name=axes, split_axis=0, concat_axis=0, tiled=True
    )
    asked, ranks, span = ask(
        valid_count,
        cand_count,
        cluster_ids,
        cluster_home.reshape(-1, LANES),
        devices,
        per_pair,
        rows_dev,
    )
    asked_here = exchange(asked)
    early = per_pair // 2
    in_blocks = lambda places: -(-places // BLOCK) * BLOCK
    totals = sorted({in_blocks(3 * per_pair // 4), in_blocks(7 * per_pair // 8), in_blocks(per_pair + 1)})
    lookup = (asked_here, store_rows, cluster_logsize.reshape(-1, LANES))
    (early_here,) = serve(*lookup, 0, [early], True)
    late_here = serve(*lookup, early, [total - early for total in totals], False)
    needed = jnp.max(asked_here[:, 0] // HIGH) + 1
    early_rows = exchange(early_here)

    weights = (
        query_proj,
        key_proj,
        value_proj,
        out_proj,
        mlp_first,
        bias_first.reshape(1, -1),
        mlp_second,
        bias_second.reshape(1, -1),
        score_proj.reshape(1, -1),
    )
    table = jnp.zeros((scorers * span_live // LANES, LANES), jnp.float32)
    scalars = (valid_count, cand_count, span)
    shared = (scalars, candidates, ranks, candidate_row)

    def finish(late_here, early_rows):
        late_rows = exchange(late_here)
        done = score(*shared, (early_rows,), weights, table, (0, early))
        return score(
            *shared, (early_rows, late_rows), weights, done, (early, early + late_here.shape[1])
        )

    level = sum((needed > total).astype(jnp.int32) for total in totals[:-1])
    branches = [
        lambda late, rows, i=i: finish(late[i], rows) for i in range(len(totals))
    ]
    table = lax.switch(level, branches, tuple(late_here), early_rows)
    parts = lax.all_to_all(
        table.reshape(scorers, span_live // LANES, LANES),
        "scorer",
        split_axis=0,
        concat_axis=0,
        tiled=True,
    )
    return jnp.sum(parts, axis=0).reshape(span_live)


def solution(mesh):
    rows = P(("store", "scorer"))
    in_specs = (
        P(("store", "scorer"), None),
        rows,
        P(),
        P(("store", "scorer"), None),
        rows,
        P(("store", "scorer"), None, None),
        rows,
        P(("store", "scorer"), None),
    ) + (P(),) * 9
    return jax.shard_map(
        on_device, mesh=mesh, in_specs=in_specs, out_specs=rows, check_vma=False
    )
```

```python
import functools
import math

import jax
import jax.numpy as jnp
from jax import lax
from jax.experimental import pallas as pl
from jax.experimental.pallas import tpu as pltpu
from jax.sharding import PartitionSpec as P

HEADS = 4
LANES = 128
BLOCK = 16
DEAD = -1e30
HIGH = 65536
VMEM_LIMIT = 40 * 1024 * 1024


def dot(a, b):
    return jnp.dot(a, b, preferred_element_type=jnp.float32)


def dot_nt(a, b):
    return lax.dot_general(a, b, (((1,), (1,)), ((), ())), preferred_element_type=jnp.float32)


def hot(mask):
    return jnp.where(mask, 1.0, 0.0).astype(jnp.bfloat16)


def iota(shape, axis):
    return lax.broadcasted_iota(jnp.int32, shape, axis)


def whole(memory_space=pltpu.VMEM):
    return pl.BlockSpec(memory_space=memory_space)


def look_up(table_t, index, pieces):
    highs = table_t.shape[1]
    count = index.shape[1]
    rows = dot(table_t, hot(iota((highs, count), 0) == (index >> 7)))
    mine = iota((LANES, count), 0) == (index & (LANES - 1))
    found = jnp.zeros((1, count), jnp.float32)
    for piece in range(pieces):
        part = rows[piece * LANES : (piece + 1) * LANES]
        found = found + float(256**piece) * jnp.sum(
            jnp.where(mine, part, 0.0), axis=0, keepdims=True
        )
    return found


def ask_kernel(
    valid_ref, count_ref, ids_ref, home_ref, asked_ref, rank_ref, span_ref, table_ref, *, rows_dev
):
    requests, slots = ids_ref.shape
    devices, per_pair = asked_ref.shape
    pieces = table_ref.shape[0] // LANES
    for piece in range(pieces):
        part = (home_ref[...] >> (8 * piece)) & 255
        table_ref[piece * LANES : (piece + 1) * LANES, :] = jnp.transpose(
            part.astype(jnp.float32)
        ).astype(jnp.bfloat16)
    table = table_ref[...]
    upto = hot(iota((slots, slots), 0) <= iota((slots, slots), 1))
    carry = jnp.zeros((devices, 1), jnp.float32)
    asked = jnp.zeros((devices, 2 * per_pair), jnp.float32)
    for r in range(requests):
        row = look_up(table, ids_ref[r : r + 1, :], pieces).astype(jnp.int32)
        dev = row // rows_dev
        local = row - dev * rows_dev
        live = iota((1, slots), 1) < jnp.where(count_ref[r] > 0, valid_ref[r], 0)
        dest = jnp.where((iota((devices, slots), 0) == dev) & live, 1.0, 0.0)
        running = dot(dest.astype(jnp.bfloat16), upto) + carry
        carry = running[:, slots - 1 : slots]
        rank_f = jnp.sum(dest * running, axis=0, keepdims=True) - 1.0
        rank = rank_f.astype(jnp.int32)
        at_rank = iota((per_pair, slots), 0) == rank
        local_f = local.astype(jnp.float32)
        high_f = (local >> 8).astype(jnp.float32)
        low_f = local_f - 256.0 * high_f
        values = jnp.concatenate(
            [jnp.where(at_rank, low_f, 0.0), jnp.where(at_rank, high_f, 0.0)], axis=0
        )
        asked = asked + dot_nt(dest.astype(jnp.bfloat16), values.astype(jnp.bfloat16))
        rank_ref[r : r + 1, :] = jnp.where(live, dev * LANES + rank, -1)
        span_ref[r] = jnp.min(jnp.where(live, rank_f, 1e9)).astype(jnp.int32)
        span_ref[requests + r] = jnp.max(rank_f).astype(jnp.int32)
    most = jnp.max(carry, axis=0, keepdims=True)
    asked = asked[:, :per_pair] + 256.0 * asked[:, per_pair:] + HIGH * most
    asked_ref[...] = asked.astype(jnp.int32)


def ask(valid_count, cand_count, cluster_ids, home_table, devices, per_pair, rows_dev):
    requests, slots = cluster_ids.shape
    highs = home_table.shape[0]
    pieces = -(-(highs * LANES - 1).bit_length() // 8)
    return pl.pallas_call(
        functools.partial(ask_kernel, rows_dev=rows_dev),
        in_specs=[whole(pltpu.SMEM), whole(pltpu.SMEM), whole(), whole()],
        out_specs=[whole(), whole(), whole(pltpu.SMEM)],
        out_shape=[
            jax.ShapeDtypeStruct((devices, per_pair), jnp.int32),
            jax.ShapeDtypeStruct((requests, slots), jnp.int32),
            jax.ShapeDtypeStruct((2 * requests,), jnp.int32),
        ],
        scratch_shapes=[pltpu.VMEM((pieces * LANES, highs), jnp.bfloat16)],
        compiler_params=pltpu.CompilerParams(vmem_limit_bytes=VMEM_LIMIT),
        cost_estimate=pl.CostEstimate(
            flops=4_000_000_000, bytes_accessed=1_000_000, transcendentals=0
        ),
        name="ask",
    )(valid_count, cand_count, cluster_ids, home_table)


def serve_kernel(asked_ref, store_ref, size_ref, *refs, first, sized):
    out_refs, column_ref = refs[:-1], refs[-1]
    devices, per_pair = asked_ref.shape
    rows_dev, width = store_ref.shape
    places = max(out_ref.shape[1] for out_ref in out_refs)
    asked = asked_ref[...] & (HIGH - 1)
    column_ref[...] = jnp.zeros(column_ref.shape, jnp.int32)
    column_ref[1 : per_pair + 1, :] = jnp.transpose(asked.astype(jnp.float32)).astype(jnp.int32)
    group = math.gcd(devices, 1 << (384 // places).bit_length() - 1)
    store = store_ref[...]
    lanes = iota((places, rows_dev), 1)
    if sized:
        size_t = jnp.transpose(size_ref[...].astype(jnp.float32)).astype(jnp.bfloat16)
    for start in range(0, devices, group):
        picks = []
        for d in range(start, start + group):
            column = column_ref[first : first + places, d : d + 1]
            picks.append(hot(column == lanes))
        found = dot(jnp.concatenate(picks, axis=0), store).reshape(group, places, width)
        if sized:
            asked_of = [asked[d : d + 1, :] for d in range(start, start + group)]
            sizes = look_up(size_t, jnp.concatenate(asked_of, axis=1), 1)
            rest = jnp.zeros((1, width - per_pair), jnp.float32)
            for g in range(group):
                mine = sizes[:, g * per_pair : (g + 1) * per_pair]
                mine = jnp.concatenate([mine, rest], axis=1)
                top = jnp.where(iota((places, width), 0) == 0, mine, found[g])
                out_refs[0][start + g] = top.astype(jnp.bfloat16)
        else:
            found = found.astype(jnp.bfloat16)
            for out_ref in out_refs:
                out_ref[start : start + group] = found[:, : out_ref.shape[1], :]


def serve(asked_here, store_rows, size_table, first, place_counts, sized):
    devices, per_pair = asked_here.shape
    rows_dev, width = store_rows.shape
    places = max(place_counts)
    column_rows = max(first + places, -(-(per_pair + 1) // BLOCK) * BLOCK)
    return pl.pallas_call(
        functools.partial(serve_kernel, first=first, sized=sized),
        in_specs=[whole(), whole(), whole()],
        out_specs=[whole() for _ in place_counts],
        out_shape=[
            jax.ShapeDtypeStruct((devices, count, width), jnp.bfloat16) for count in place_counts
        ],
        scratch_shapes=[pltpu.VMEM((column_rows, devices), jnp.int32)],
        compiler_params=pltpu.CompilerParams(vmem_limit_bytes=VMEM_LIMIT),
        cost_estimate=pl.CostEstimate(
            flops=2 * devices * places * rows_dev * width,
            bytes_accessed=2 * (rows_dev + devices * sum(place_counts)) * width,
            transcendentals=0,
        ),
        name="serve",
    )(asked_here, store_rows, size_table)


def column_of(row):
    return jnp.transpose(jnp.broadcast_to(row, (LANES, row.shape[1])))


def row_of(ref, r, columns):
    part = ref[:, columns]
    mine = jnp.where(iota(part.shape, 0) == r, part.astype(jnp.float32), 0.0)
    return jnp.sum(mine, axis=0, keepdims=True).astype(jnp.int32)


def prep_kernel(
    cand_ref,
    query_ref,
    value_ref,
    out_proj_ref,
    first_ref,
    bias_first_ref,
    second_ref,
    bias_second_ref,
    after_ref,
    cand_t_ref,
    query_t_ref,
    value_t_ref,
    out_proj_t_ref,
    first_t_ref,
    bias_first_t_ref,
    second_t_ref,
    bias_second_t_ref,
):
    del after_ref
    pairs = (
        (value_ref, value_t_ref),
        (out_proj_ref, out_proj_t_ref),
        (first_ref, first_t_ref),
        (second_ref, second_t_ref),
    )
    for ref, ref_t in pairs:
        ref_t[...] = jnp.transpose(ref[...].astype(jnp.float32)).astype(jnp.bfloat16)
    bias_first_t_ref[...] = column_of(bias_first_ref[...])
    bias_second_t_ref[...] = column_of(bias_second_ref[...])
    query_t = jnp.transpose(query_ref[...].astype(jnp.float32)).astype(jnp.bfloat16)

    def one_request(r, carry):
        cand_t = jnp.transpose(cand_ref[r].astype(jnp.float32)).astype(jnp.bfloat16)
        cand_t_ref[r] = cand_t
        query_t_ref[r] = dot(query_t, cand_t).astype(jnp.bfloat16)
        return carry

    lax.fori_loop(0, cand_ref.shape[0], one_request, 0)


def prep(candidates, weights, after):
    requests, cands, width = candidates.shape
    query_proj, value_proj, out_proj, mlp_first, bias_first, mlp_second, bias_second = weights
    turned = lambda x: jax.ShapeDtypeStruct(x.shape[::-1], jnp.bfloat16)
    column = lambda x: jax.ShapeDtypeStruct((x.shape[1], LANES), jnp.float32)
    cands_t = jax.ShapeDtypeStruct((requests, width, cands), jnp.bfloat16)
    return pl.pallas_call(
        prep_kernel,
        in_specs=[whole() for _ in range(8)] + [whole(pl.ANY)],
        out_specs=[whole() for _ in range(8)],
        out_shape=[
            cands_t,
            cands_t,
            turned(value_proj),
            turned(out_proj),
            turned(mlp_first),
            column(bias_first),
            turned(mlp_second),
            column(bias_second),
        ],
        compiler_params=pltpu.CompilerParams(vmem_limit_bytes=VMEM_LIMIT),
        cost_estimate=pl.CostEstimate(
            flops=2 * requests * cands * width * width,
            bytes_accessed=6 * requests * cands * width,
            transcendentals=0,
        ),
        name="prep",
    )(candidates, *weights, after)


def score_kernel(*refs, bases, from_place, to_place):
    valid_ref, count_ref, span_ref, cand_ref, query_ref, rank_ref, target_ref = refs[:7]
    arrived_refs = refs[7 : 7 + len(bases)]
    (
        key_ref,
        value_ref,
        out_proj_ref,
        first_ref,
        bias_first_ref,
        second_ref,
        bias_second_ref,
        score_ref,
        before_ref,
        table_ref,
        rows_ref,
        keys_ref,
        values_ref,
        offset_ref,
        size_ref,
    ) = refs[7 + len(bases) :]
    requests, slots = rank_ref.shape
    devices = arrived_refs[0].shape[0]
    width, cands = cand_ref.shape[1:]
    head_size = width // HEADS
    cand_part = math.gcd(cands, 256)
    highs = table_ref.shape[0]
    to_exp2 = math.log2(math.e) / math.sqrt(head_size)
    wide = lambda column, lanes: jnp.concatenate([column] * (lanes // LANES), axis=1)

    table_ref[...] = before_ref[...]
    heads_of = arrived_refs[0][:, :BLOCK, :LANES].astype(jnp.float32)
    at_top = iota(heads_of.shape, 1) == 0
    sizes = jnp.sum(jnp.where(at_top, heads_of, 0.0), axis=1)
    size_ref[...] = jnp.transpose(sizes).astype(jnp.bfloat16)

    def run(r, n):
        count = count_ref[r]
        low_block = (span_ref[r] + 1) // BLOCK
        high_block = (span_ref[requests + r] + 1) // BLOCK
        spot = row_of(rank_ref, r, slice(0, n))
        at = (spot & (LANES - 1)) + 1
        place = (at // BLOCK) * (devices * BLOCK) + (spot // LANES) * BLOCK + at % BLOCK
        place = column_of(jnp.where(spot >= 0, place, -1))
        offset = look_up(size_ref[...], spot, 1) * math.sqrt(head_size)
        offset_ref[:n, :] = column_of(jnp.where(spot >= 0, offset, DEAD))
        rows_ref[:n, :] = jnp.zeros((n, width), jnp.float32)
        for arrived_ref, base in zip(arrived_refs, bases):
            block_rows = devices * BLOCK
            blocks = arrived_ref.shape[1] // BLOCK

            def add_block(j, carry):
                start = pl.multiple_of(j * BLOCK, BLOCK)
                block = arrived_ref[:, pl.ds(start, BLOCK), :].reshape(block_rows, width)
                rel = place - (j + base) * block_rows
                lanes = iota((n, LANES), 1)
                picks = [hot(rel == lanes + g * LANES) for g in range(block_rows // LANES)]
                rows_ref[:n, :] += dot(jnp.concatenate(picks, axis=1), block)
                return carry

            lax.fori_loop(
                jnp.clip(low_block - base, 0, blocks),
                jnp.clip(high_block + 1 - base, 0, blocks),
                add_block,
                0,
            )
        rows = rows_ref[:n, :].astype(jnp.bfloat16)
        keys = dot(rows, key_ref[...]).astype(jnp.bfloat16)
        for h in range(HEADS):
            keys_ref[h, :n, :] = keys[:, h * head_size : (h + 1) * head_size]
        values_ref[:, :n] = dot_nt(value_ref[...], rows).astype(jnp.bfloat16)

        def part(c, carry):
            start = pl.multiple_of(c * cand_part, cand_part)
            columns = pl.ds(start, cand_part)
            context = []
            for h in range(HEADS):
                head = slice(h * head_size, (h + 1) * head_size)
                logits = dot(keys_ref[h, :n, :], query_ref[r, head, columns])
                logits = logits + wide(offset_ref[:n, :], cand_part)
                top = jnp.max(logits, axis=0, keepdims=True)
                weights = jnp.exp2((logits - top) * to_exp2)
                probs = weights * (1.0 / jnp.sum(weights, axis=0, keepdims=True))
                context.append(dot(values_ref[head, :n], probs.astype(jnp.bfloat16)))
            context = jnp.concatenate(context, axis=0).astype(jnp.bfloat16)
            attended = dot(out_proj_ref[...], context).astype(jnp.bfloat16)
            hidden = (
                dot(first_ref[:, :width], cand_ref[r, :, columns])
                + dot(first_ref[:, width:], attended)
                + wide(bias_first_ref[...], cand_part)
            )
            hidden = jnp.maximum(hidden, 0.0).astype(jnp.bfloat16)
            hidden = dot(second_ref[...], hidden) + wide(bias_second_ref[...], cand_part)
            hidden = jnp.maximum(hidden, 0.0).astype(jnp.bfloat16)
            scores = dot(jnp.broadcast_to(score_ref[...], (8, hidden.shape[0])), hidden)[:1]
            target = row_of(target_ref, r, columns)
            counted = iota((1, cand_part), 1) + start < count
            high_hot = hot((iota((highs, cand_part), 0) == (target >> 7)) & counted)
            at_low = iota((LANES, cand_part), 0) == (target & (LANES - 1))
            left = scores
            for _ in range(3):
                piece = left.astype(jnp.bfloat16).astype(jnp.float32)
                left = left - piece
                table_ref[...] += dot_nt(
                    high_hot, jnp.where(at_low, piece, 0.0).astype(jnp.bfloat16)
                )
            return carry

        lax.fori_loop(0, (count + cand_part - 1) // cand_part, part, 0)

    def one_request(r, carry):
        valid = valid_ref[r]
        last_place = span_ref[requests + r] + 1
        mine = (count_ref[r] > 0) & (last_place >= from_place) & (last_place < to_place)
        for n in range(LANES, slots + 1, LANES):

            @pl.when(mine & (valid > n - LANES) & (valid <= n))
            def _():
                run(r, n)

        return carry

    lax.fori_loop(0, requests, one_request, 0)


def score(scalars, operands, arrived, weights, before, places):
    cands_t, _, ranks, _ = operands
    width = cands_t.shape[1]
    slots = ranks.shape[1]
    devices = arrived[0].shape[0]
    bases = (0, arrived[0].shape[1] // BLOCK)[: len(arrived)]
    operands = [*operands, *arrived, *weights, before]
    return pl.pallas_call(
        functools.partial(score_kernel, bases=bases, from_place=places[0], to_place=places[1]),
        in_specs=[whole(pltpu.SMEM)] * 3 + [whole() for _ in operands],
        out_specs=whole(),
        scratch_shapes=[
            pltpu.VMEM((slots, width), jnp.float32),
            pltpu.VMEM((HEADS, slots, width // HEADS), jnp.bfloat16),
            pltpu.VMEM((width, slots), jnp.bfloat16),
            pltpu.VMEM((slots, LANES), jnp.float32),
            pltpu.VMEM((LANES, devices), jnp.bfloat16),
        ],
        out_shape=jax.ShapeDtypeStruct(before.shape, jnp.float32),
        compiler_params=pltpu.CompilerParams(vmem_limit_bytes=VMEM_LIMIT),
        cost_estimate=pl.CostEstimate(
            flops=10_000_000_000, bytes_accessed=5_000_000, transcendentals=4_000_000
        ),
        name="score",
    )(*scalars, *operands)


def on_device(
    store_rows,
    cluster_logsize,
    cluster_home,
    cluster_ids,
    valid_count,
    candidates,
    cand_count,
    candidate_row,
    query_proj,
    key_proj,
    value_proj,
    out_proj,
    mlp_first,
    bias_first,
    mlp_second,
    bias_second,
    score_proj,
):
    axes = ("store", "scorer")
    devices = lax.axis_size(axes)
    scorers = lax.axis_size("scorer")
    requests, slots = cluster_ids.shape
    rows_dev, width = store_rows.shape
    cands = candidates.shape[1]
    per_pair = requests * slots // devices
    span_live = requests * cands // 2

    exchange = functools.partial(
        lax.all_to_all, axis_name=axes, split_axis=0, concat_axis=0, tiled=True
    )
    asked, ranks, span = ask(
        valid_count,
        cand_count,
        cluster_ids,
        cluster_home.reshape(-1, LANES),
        devices,
        per_pair,
        rows_dev,
    )
    asked_here = exchange(asked)
    in_blocks = lambda places: -(-places // BLOCK) * BLOCK
    early = in_blocks(per_pair // 2 + 1) if per_pair >= 8 * BLOCK else BLOCK
    totals = sorted({in_blocks(3 * per_pair // 4), in_blocks(7 * per_pair // 8), in_blocks(per_pair + 1)})
    lookup = (asked_here, store_rows, cluster_logsize.reshape(-1, LANES))
    (early_here,) = serve(*lookup, 0, [early], True)
    late_here = serve(*lookup, early, [total - early for total in totals], False)
    needed = jnp.max(asked_here[:, 0] // HIGH) + 1
    early_rows = exchange(early_here)

    turning = (
        query_proj,
        value_proj,
        out_proj,
        mlp_first,
        bias_first.reshape(1, -1),
        mlp_second,
        bias_second.reshape(1, -1),
    )
    cands_t, queries_t, *turned = prep(candidates, turning, early_here)
    weights = (key_proj, *turned, score_proj.reshape(1, -1))
    table = jnp.zeros((scorers * span_live // LANES, LANES), jnp.float32)
    scalars = (valid_count, cand_count, span)
    shared = (scalars, (cands_t, queries_t, ranks, candidate_row))

    def finish(late_here, early_rows):
        late_rows = exchange(late_here)
        done = score(*shared, (early_rows,), weights, table, (0, early))
        return score(
            *shared, (early_rows, late_rows), weights, done, (early, early + late_here.shape[1])
        )

    level = sum((needed > total).astype(jnp.int32) for total in totals[:-1])
    branches = [
        lambda late, rows, i=i: finish(late[i], rows) for i in range(len(totals))
    ]
    table = lax.switch(level, branches, tuple(late_here), early_rows)
    parts = lax.all_to_all(
        table.reshape(scorers, span_live // LANES, LANES),
        "scorer",
        split_axis=0,
        concat_axis=0,
        tiled=True,
    )
    return jnp.sum(parts, axis=0).reshape(span_live)


def solution(mesh):
    rows = P(("store", "scorer"))
    in_specs = (
        P(("store", "scorer"), None),
        rows,
        P(),
        P(("store", "scorer"), None),
        rows,
        P(("store", "scorer"), None, None),
        rows,
        P(("store", "scorer"), None),
    ) + (P(),) * 9
    return jax.shard_map(
        on_device, mesh=mesh, in_specs=in_specs, out_specs=rows, check_vma=False
    )
```

```python
import functools
import math

import jax
import jax.numpy as jnp
from jax import lax
from jax.experimental import pallas as pl
from jax.experimental.pallas import tpu as pltpu
from jax.sharding import PartitionSpec as P

HEADS = 4
LANES = 128
BLOCK = 16
DEAD = -1e30
HIGH = 65536
OFFSET_PIECES = 3
ROWS_AT_ONCE = 64
SUM_LEAST = 2.0**-100
SUM_MOST = 2.0**100
VMEM_LIMIT = 40 * 1024 * 1024


def dot(a, b):
    return jnp.dot(a, b, preferred_element_type=jnp.float32)


def dot_nt(a, b):
    return lax.dot_general(a, b, (((1,), (1,)), ((), ())), preferred_element_type=jnp.float32)


def hot(mask):
    return jnp.where(mask, 1.0, 0.0).astype(jnp.bfloat16)


def iota(shape, axis):
    return lax.broadcasted_iota(jnp.int32, shape, axis)


def whole(memory_space=pltpu.VMEM):
    return pl.BlockSpec(memory_space=memory_space)


def look_up(table_t, index, pieces):
    highs = table_t.shape[1]
    count = index.shape[1]
    rows = dot(table_t, hot(iota((highs, count), 0) == (index >> 7)))
    mine = iota((LANES, count), 0) == (index & (LANES - 1))
    found = jnp.zeros((1, count), jnp.float32)
    for piece in range(pieces):
        part = rows[piece * LANES : (piece + 1) * LANES]
        found = found + float(256**piece) * jnp.sum(
            jnp.where(mine, part, 0.0), axis=0, keepdims=True
        )
    return found


def ask_kernel(
    valid_ref, count_ref, ids_ref, home_ref, asked_ref, rank_ref, span_ref, table_ref, *, rows_dev
):
    requests, slots = ids_ref.shape
    devices, per_pair = asked_ref.shape
    pieces = table_ref.shape[0] // LANES
    for piece in range(pieces):
        part = (home_ref[...] >> (8 * piece)) & 255
        table_ref[piece * LANES : (piece + 1) * LANES, :] = jnp.transpose(
            part.astype(jnp.float32)
        ).astype(jnp.bfloat16)
    table = table_ref[...]
    upto = hot(iota((slots, slots), 0) <= iota((slots, slots), 1))
    carry = jnp.zeros((devices, 1), jnp.float32)
    asked = jnp.zeros((devices, 2 * per_pair), jnp.float32)
    for r in range(requests):
        row = look_up(table, ids_ref[r : r + 1, :], pieces).astype(jnp.int32)
        dev = row // rows_dev
        local = row - dev * rows_dev
        live = iota((1, slots), 1) < jnp.where(count_ref[r] > 0, valid_ref[r], 0)
        dest = jnp.where((iota((devices, slots), 0) == dev) & live, 1.0, 0.0)
        running = dot(dest.astype(jnp.bfloat16), upto) + carry
        carry = running[:, slots - 1 : slots]
        rank_f = jnp.sum(dest * running, axis=0, keepdims=True) - 1.0
        rank = rank_f.astype(jnp.int32)
        at_rank = iota((per_pair, slots), 0) == rank
        local_f = local.astype(jnp.float32)
        high_f = (local >> 8).astype(jnp.float32)
        low_f = local_f - 256.0 * high_f
        values = jnp.concatenate(
            [jnp.where(at_rank, low_f, 0.0), jnp.where(at_rank, high_f, 0.0)], axis=0
        )
        asked = asked + dot_nt(dest.astype(jnp.bfloat16), values.astype(jnp.bfloat16))
        rank_ref[r : r + 1, :] = jnp.where(live, dev * LANES + rank, -1)
        span_ref[r] = jnp.min(jnp.where(live, rank_f, 1e9)).astype(jnp.int32)
        span_ref[requests + r] = jnp.max(rank_f).astype(jnp.int32)
    most = jnp.max(carry, axis=0, keepdims=True)
    asked = asked[:, :per_pair] + 256.0 * asked[:, per_pair:] + HIGH * most
    asked_ref[...] = asked.astype(jnp.int32)


def ask(valid_count, cand_count, cluster_ids, home_table, devices, per_pair, rows_dev):
    requests, slots = cluster_ids.shape
    highs = home_table.shape[0]
    pieces = -(-(highs * LANES - 1).bit_length() // 8)
    return pl.pallas_call(
        functools.partial(ask_kernel, rows_dev=rows_dev),
        in_specs=[whole(pltpu.SMEM), whole(pltpu.SMEM), whole(), whole()],
        out_specs=[whole(), whole(), whole(pltpu.SMEM)],
        out_shape=[
            jax.ShapeDtypeStruct((devices, per_pair), jnp.int32),
            jax.ShapeDtypeStruct((requests, slots), jnp.int32),
            jax.ShapeDtypeStruct((2 * requests,), jnp.int32),
        ],
        scratch_shapes=[pltpu.VMEM((pieces * LANES, highs), jnp.bfloat16)],
        compiler_params=pltpu.CompilerParams(vmem_limit_bytes=VMEM_LIMIT),
        cost_estimate=pl.CostEstimate(
            flops=4_000_000_000, bytes_accessed=1_000_000, transcendentals=0
        ),
        name="ask",
    )(valid_count, cand_count, cluster_ids, home_table)


def serve_kernel(asked_ref, store_ref, size_ref, after_ref, *refs, first, sized):
    del after_ref
    out_refs, column_ref = refs[:-1], refs[-1]
    devices, per_pair = asked_ref.shape
    rows_dev, width = store_ref.shape
    places = max(out_ref.shape[1] for out_ref in out_refs)
    asked = asked_ref[...] & (HIGH - 1)
    column_ref[...] = jnp.zeros(column_ref.shape, jnp.int32)
    column_ref[1 : per_pair + 1, :] = jnp.transpose(asked.astype(jnp.float32)).astype(jnp.int32)
    group = math.gcd(devices, 1 << (384 // places).bit_length() - 1)
    store = store_ref[...]
    lanes = iota((places, rows_dev), 1)
    if sized:
        size_t = jnp.transpose(size_ref[...].astype(jnp.float32)).astype(jnp.bfloat16)
    for start in range(0, devices, group):
        picks = []
        for d in range(start, start + group):
            column = column_ref[first : first + places, d : d + 1]
            picks.append(hot(column == lanes))
        found = dot(jnp.concatenate(picks, axis=0), store).reshape(group, places, width)
        if sized:
            asked_of = [asked[d : d + 1, :] for d in range(start, start + group)]
            sizes = look_up(size_t, jnp.concatenate(asked_of, axis=1), 1)
            rest = jnp.zeros((1, width - per_pair), jnp.float32)
            for g in range(group):
                mine = sizes[:, g * per_pair : (g + 1) * per_pair]
                mine = jnp.concatenate([mine, rest], axis=1)
                top = jnp.where(iota((places, width), 0) == 0, mine, found[g])
                out_refs[0][start + g] = top.astype(jnp.bfloat16)
        else:
            found = found.astype(jnp.bfloat16)
            for out_ref in out_refs:
                out_ref[start : start + group] = found[:, : out_ref.shape[1], :]


def serve(asked_here, store_rows, size_table, after, first, place_counts, sized):
    devices, per_pair = asked_here.shape
    rows_dev, width = store_rows.shape
    places = max(place_counts)
    column_rows = max(first + places, -(-(per_pair + 1) // BLOCK) * BLOCK)
    return pl.pallas_call(
        functools.partial(serve_kernel, first=first, sized=sized),
        in_specs=[whole(), whole(), whole(), whole(pl.ANY)],
        out_specs=[whole() for _ in place_counts],
        out_shape=[
            jax.ShapeDtypeStruct((devices, count, width), jnp.bfloat16) for count in place_counts
        ],
        scratch_shapes=[pltpu.VMEM((column_rows, devices), jnp.int32)],
        compiler_params=pltpu.CompilerParams(vmem_limit_bytes=VMEM_LIMIT),
        cost_estimate=pl.CostEstimate(
            flops=2 * devices * places * rows_dev * width,
            bytes_accessed=2 * (rows_dev + devices * sum(place_counts)) * width,
            transcendentals=0,
        ),
        name="serve",
    )(asked_here, store_rows, size_table, after)


def column_of(row):
    return jnp.transpose(jnp.broadcast_to(row, (LANES, row.shape[1])))


def row_of(ref, r, columns):
    part = ref[:, columns]
    mine = jnp.where(iota(part.shape, 0) == r, part.astype(jnp.float32), 0.0)
    return jnp.sum(mine, axis=0, keepdims=True).astype(jnp.int32)


def prep_kernel(cand_ref, query_ref, score_ref, rank_ref, after_ref, *out_refs):
    queries_ref, place_ref, score_cols_ref = out_refs
    devices = after_ref.shape[0]
    cands, width = cand_ref.shape[1:]
    size = width // HEADS
    lane = iota((cands, LANES), 1)
    score = jnp.broadcast_to(score_ref[...].astype(jnp.float32), (LANES, score_ref.shape[1]))
    score_cols_ref[...] = jnp.transpose(score).astype(jnp.bfloat16)

    def one_request(r, carry):
        queries = dot(cand_ref[r], query_ref[...])
        for h in range(HEADS):
            pair = queries[:, h // 2 * LANES : (h // 2 + 1) * LANES]
            own = lane // size == h % 2
            picks = jnp.where(lane % size < OFFSET_PIECES, 1.0, 0.0)
            queries_ref[r, h] = jnp.where(own, pair, picks).astype(jnp.bfloat16)
        spot = row_of(rank_ref, r, slice(None))
        at = (spot & (LANES - 1)) + 1
        place = (at // BLOCK) * (devices * BLOCK) + (spot // LANES) * BLOCK + at % BLOCK
        place_ref[r] = column_of(jnp.where(spot >= 0, place, -1))
        return carry

    lax.fori_loop(0, cand_ref.shape[0], one_request, 0)


def prep(candidates, query_proj, score_proj, ranks, after):
    requests, cands, width = candidates.shape
    return pl.pallas_call(
        prep_kernel,
        in_specs=[whole() for _ in range(4)] + [whole(pl.ANY)],
        out_specs=[whole() for _ in range(3)],
        out_shape=[
            jax.ShapeDtypeStruct((requests, HEADS, cands, LANES), jnp.bfloat16),
            jax.ShapeDtypeStruct((*ranks.shape, LANES), jnp.int32),
            jax.ShapeDtypeStruct((score_proj.shape[1], LANES), jnp.bfloat16),
        ],
        compiler_params=pltpu.CompilerParams(vmem_limit_bytes=VMEM_LIMIT),
        cost_estimate=pl.CostEstimate(
            flops=2 * requests * cands * width * width,
            bytes_accessed=10 * requests * cands * width,
            transcendentals=0,
        ),
        name="prep",
    )(candidates, query_proj, score_proj, ranks, after)


def score_kernel(*refs, bases, from_place, to_place, exact):
    valid_ref, count_ref, span_ref = refs[:3]
    cand_all, queries_all, place_all, rank_ref, target_ref = refs[3:8]
    arrived_all = refs[8 : 8 + len(bases)]
    (
        key_ref,
        value_ref,
        out_proj_ref,
        first_ref,
        bias_first_ref,
        second_ref,
        bias_second_ref,
        score_ref,
        before_ref,
        table_ref,
        flag_ref,
        rows_ref,
        keys_ref,
        values_ref,
        context_ref,
        least_ref,
        most_ref,
        size_ref,
        cand_ref,
        queries_ref,
        place_ref,
        arrived_sems,
        request_sems,
        *arrived_refs,
    ) = refs[8 + len(bases) :]
    requests, slots = rank_ref.shape
    devices = arrived_refs[0].shape[0]
    cands, width = cand_ref.shape[1:]
    head_size = width // HEADS
    cand_part = math.gcd(cands, 256)
    highs = table_ref.shape[0]
    scale = math.sqrt(head_size)
    to_log2 = math.log2(math.e) / scale
    sizes_done = [slots] if exact else range(slots // 2, slots + 1, LANES)
    fetched = ((place_all, place_ref), (queries_all, queries_ref), (cand_all, cand_ref))
    own_rows = [slice(h % 2 * head_size, (h % 2 + 1) * head_size) for h in range(HEADS)]
    other_rows = [slice((1 - h % 2) * head_size, (2 - h % 2) * head_size) for h in range(HEADS)]

    def is_mine(r):
        last_place = span_ref[requests + r] + 1
        return (count_ref[r] > 0) & (last_place >= from_place) & (last_place < to_place)

    def copies_of(r):
        return [
            pltpu.make_async_copy(source.at[r], target.at[r], request_sems.at[i, r])
            for i, (source, target) in enumerate(fetched)
        ]

    arrivals = [
        pltpu.make_async_copy(source, target, arrived_sems.at[i])
        for i, (source, target) in enumerate(zip(arrived_all, arrived_refs))
    ]
    for copy in arrivals:
        copy.start()
    for r in range(requests):

        @pl.when(is_mine(r))
        def _():
            for copy in copies_of(r):
                copy.start()

    keys_ref[...] = jnp.zeros(keys_ref.shape, jnp.bfloat16)
    values_ref[...] = jnp.zeros(values_ref.shape, jnp.bfloat16)
    for copy in arrivals:
        copy.wait()
    heads_of = arrived_refs[0][:, :BLOCK, :LANES].astype(jnp.float32)
    at_top = iota(heads_of.shape, 1) == 0
    sizes = jnp.sum(jnp.where(at_top, heads_of, 0.0), axis=1)
    size_ref[...] = jnp.transpose(sizes).astype(jnp.bfloat16)

    def select(r, n, arrived_ref, base):
        block_rows = devices * BLOCK
        blocks = arrived_ref.shape[1] // BLOCK
        at_once = min(2, blocks)
        low_block = jnp.clip((span_ref[r] + 1) // BLOCK - base, 0, blocks)
        high_block = jnp.clip((span_ref[requests + r] + 1) // BLOCK + 1 - base, 0, blocks)

        def step(i, carry):
            wanted = low_block + i * at_once
            j = jnp.minimum(wanted, blocks - at_once)
            place = place_ref[r, :n, :]
            rel = jnp.where(place >= (wanted + base) * block_rows, place, -1)
            rel = rel - (j + base) * block_rows
            lanes = iota((n, LANES), 1)
            found = []
            for b in range(at_once):
                start = pl.multiple_of((j + b) * BLOCK, BLOCK)
                block = arrived_ref[:, pl.ds(start, BLOCK), :].reshape(block_rows, width)
                firsts = range(b * block_rows, (b + 1) * block_rows, LANES)
                picks = [hot(rel == lanes + first) for first in firsts]
                found.append(dot(jnp.concatenate(picks, axis=1), block))
            rows_ref[:n, :] += sum(found)
            return carry

        lax.fori_loop(0, (high_block - low_block + at_once - 1) // at_once, step, 0)

    def load(r, n):
        rows_ref[:n, :] = jnp.zeros((n, width), jnp.float32)
        for arrived_ref, base in zip(arrived_refs, bases):
            select(r, n, arrived_ref, base)
        spot = row_of(rank_ref, r, slice(0, n))
        size = look_up(size_ref[...], spot, 1)
        largest = jnp.max(jnp.where(spot >= 0, size, DEAD), axis=1, keepdims=True)
        left = jnp.where(spot >= 0, (size - largest) * scale, DEAD)
        pieces = jnp.zeros((head_size, n), jnp.float32)
        for row in range(OFFSET_PIECES):
            piece = left.astype(jnp.bfloat16).astype(jnp.float32)
            left = left - piece
            pieces = jnp.where(iota((head_size, n), 0) == row, piece, pieces)
        pieces = pieces.astype(jnp.bfloat16)
        rows = rows_ref[:n, :].astype(jnp.bfloat16)
        keys = dot_nt(key_ref[...], rows).astype(jnp.bfloat16)
        values = dot(rows, value_ref[...])
        own = iota((n, LANES), 1) // head_size
        for h in range(HEADS):
            keys_ref[h, own_rows[h], :n] = keys[h * head_size : (h + 1) * head_size]
            keys_ref[h, other_rows[h], :n] = pieces
            if n < slots:
                rest = (head_size, slots - n)
                dead = jnp.where(iota(rest, 0) == 0, DEAD, 0.0).astype(jnp.bfloat16)
                keys_ref[h, other_rows[h], n:] = dead
            pair = values[:, h // 2 * LANES : (h // 2 + 1) * LANES]
            first = h % 2 * n
            values_ref[h // 2, first : first + n, :] = jnp.where(own == h % 2, pair, 0.0).astype(
                jnp.bfloat16
            )

    def attend(r, n, slot):
        least = least_ref[...]
        most = most_ref[...]
        for pair in range(HEADS // 2):
            probs = []
            for h in (2 * pair, 2 * pair + 1):
                logits = dot(queries_ref[r, h], keys_ref[h, :, :n])
                of_head = []
                for first in range(0, cands, ROWS_AT_ONCE):
                    weights = jnp.exp2(logits[first : first + ROWS_AT_ONCE] * to_log2)
                    total = jnp.sum(weights, axis=1, keepdims=True)
                    least = jnp.minimum(least, total)
                    most = jnp.maximum(most, total)
                    of_head.append((weights * (1.0 / total)).astype(jnp.bfloat16))
                probs.append(jnp.concatenate(of_head, axis=0))
            context = dot(jnp.concatenate(probs, axis=1), values_ref[pair, : 2 * n, :])
            context_ref[slot, :, pair * LANES : (pair + 1) * LANES] = context.astype(jnp.bfloat16)
        least_ref[...] = least
        most_ref[...] = most

    def attend_exactly(r, slot):
        def part(c, carry):
            rows = pl.ds(pl.multiple_of(c * cand_part, cand_part), cand_part)
            for pair in range(HEADS // 2):
                probs = []
                for h in (2 * pair, 2 * pair + 1):
                    logits = dot(queries_ref[r, h, rows, :], keys_ref[h])
                    top = jnp.max(logits, axis=1, keepdims=True)
                    weights = jnp.exp2((logits - top) * to_log2)
                    total = jnp.sum(weights, axis=1, keepdims=True)
                    probs.append((weights * (1.0 / total)).astype(jnp.bfloat16))
                context = dot(jnp.concatenate(probs, axis=1), values_ref[pair])
                columns = slice(pair * LANES, (pair + 1) * LANES)
                context_ref[slot, rows, columns] = context.astype(jnp.bfloat16)
            return carry

        lax.fori_loop(0, cands // cand_part, part, 0)

    def rate(last, slot):
        r = jnp.maximum(last, 0)
        attended = dot(context_ref[slot], out_proj_ref[...]).astype(jnp.bfloat16)
        hidden = (
            dot(cand_ref[r], first_ref[:width, :])
            + dot(attended, first_ref[width:, :])
            + bias_first_ref[...]
        )
        hidden = jnp.maximum(hidden, 0.0).astype(jnp.bfloat16)
        hidden = dot(hidden, second_ref[...]) + bias_second_ref[...]
        hidden = jnp.maximum(hidden, 0.0).astype(jnp.bfloat16)
        scores = jnp.transpose(dot(hidden, score_ref[...]))[:1]
        target = row_of(target_ref, r, slice(None))
        counted = iota((1, cands), 1) < jnp.where(last >= 0, count_ref[r], 0)
        high_hot = hot((iota((highs, cands), 0) == (target >> 7)) & counted)
        at_low = iota((LANES, cands), 0) == (target & (LANES - 1))
        left = jnp.where(counted, scores, 0.0)
        pieces = []
        for _ in range(3):
            piece = left.astype(jnp.bfloat16).astype(jnp.float32)
            left = left - piece
            pieces.append(jnp.where(at_low, piece, 0.0).astype(jnp.bfloat16))
        found = dot_nt(high_hot, jnp.concatenate(pieces, axis=0))
        table_ref[...] += sum(found[:, i * LANES : (i + 1) * LANES] for i in range(3))

    def one_request(r, carry):
        last, slot = carry
        valid = valid_ref[r]
        mine = is_mine(r)

        @pl.when(mine)
        def _():
            for copy in copies_of(r):
                copy.wait()
            fewer = 0
            for n in sizes_done:

                @pl.when((valid > fewer) & (valid <= n))
                def _():
                    load(r, n)
                    if exact:
                        attend_exactly(r, slot)
                        rate(r, slot)
                    else:
                        rate(last, slot)
                        attend(r, n, 1 - slot)

                fewer = n

        return jnp.where(mine, r, last), jnp.where(mine, 1 - slot, slot)

    table_ref[...] = before_ref[...]
    least_ref[...] = jnp.ones(least_ref.shape, jnp.float32)
    most_ref[...] = jnp.ones(most_ref.shape, jnp.float32)
    context_ref[...] = jnp.zeros(context_ref.shape, jnp.bfloat16)
    last, slot = lax.fori_loop(0, requests, one_request, (jnp.int32(-1), jnp.int32(0)))
    if not exact:

        @pl.when(last >= 0)
        def _():
            rate(last, slot)

    in_range = (jnp.min(least_ref[...]) >= SUM_LEAST) & (jnp.max(most_ref[...]) <= SUM_MOST)
    flag_ref[0] = jnp.where(in_range, 0, 1)


def score(scalars, operands, arrived, weights, before, places, exact=False):
    candidates, queries, columns, ranks, _ = operands
    cands, width = candidates.shape[1:]
    slots = ranks.shape[1]
    devices = arrived[0].shape[0]
    bases = []
    for rows in arrived:
        bases.append(bases[-1] + arrived[len(bases) - 1].shape[1] // BLOCK if bases else 0)
    operands = [*operands, *arrived, *weights, before]
    return pl.pallas_call(
        functools.partial(
            score_kernel,
            bases=tuple(bases),
            from_place=places[0],
            to_place=places[1],
            exact=exact,
        ),
        in_specs=[whole(pltpu.SMEM)] * 3
        + [whole(pl.ANY)] * 3
        + [whole()] * 2
        + [whole(pl.ANY)] * len(arrived)
        + [whole() for _ in (*weights, before)],
        out_specs=[whole(), whole(pltpu.SMEM)],
        scratch_shapes=[
            pltpu.VMEM((slots, width), jnp.float32),
            pltpu.VMEM((HEADS, LANES, slots), jnp.bfloat16),
            pltpu.VMEM((HEADS // 2, 2 * slots, LANES), jnp.bfloat16),
            pltpu.VMEM((2, cands, width), jnp.bfloat16),
            pltpu.VMEM((ROWS_AT_ONCE, 1), jnp.float32),
            pltpu.VMEM((ROWS_AT_ONCE, 1), jnp.float32),
            pltpu.VMEM((LANES, devices), jnp.bfloat16),
            pltpu.VMEM(candidates.shape, candidates.dtype),
            pltpu.VMEM(queries.shape, queries.dtype),
            pltpu.VMEM(columns.shape, columns.dtype),
            pltpu.SemaphoreType.DMA((len(arrived),)),
            pltpu.SemaphoreType.DMA((3, ranks.shape[0])),
            *(pltpu.VMEM(rows.shape, rows.dtype) for rows in arrived),
        ],
        out_shape=[
            jax.ShapeDtypeStruct(before.shape, jnp.float32),
            jax.ShapeDtypeStruct((1,), jnp.int32),
        ],
        compiler_params=pltpu.CompilerParams(vmem_limit_bytes=VMEM_LIMIT),
        cost_estimate=pl.CostEstimate(
            flops=10_000_000_000, bytes_accessed=5_000_000, transcendentals=4_000_000
        ),
        name="score",
    )(*scalars, *operands)


def on_device(
    store_rows,
    cluster_logsize,
    cluster_home,
    cluster_ids,
    valid_count,
    candidates,
    cand_count,
    candidate_row,
    query_proj,
    key_proj,
    value_proj,
    out_proj,
    mlp_first,
    bias_first,
    mlp_second,
    bias_second,
    score_proj,
):
    axes = ("store", "scorer")
    devices = lax.axis_size(axes)
    scorers = lax.axis_size("scorer")
    requests, slots = cluster_ids.shape
    rows_dev, width = store_rows.shape
    cands = candidates.shape[1]
    per_pair = requests * slots // devices
    span_live = requests * cands // 2

    exchange = functools.partial(
        lax.all_to_all, axis_name=axes, split_axis=0, concat_axis=0, tiled=True
    )
    asked, ranks, span = ask(
        valid_count,
        cand_count,
        cluster_ids,
        cluster_home.reshape(-1, LANES),
        devices,
        per_pair,
        rows_dev,
    )
    asked_here = exchange(asked)
    in_blocks = lambda places: -(-places // BLOCK) * BLOCK
    early = in_blocks(per_pair // 2)
    cuts = (0, early, in_blocks(7 * per_pair // 8), in_blocks(per_pair + 1))
    lookup = (asked_here, store_rows, cluster_logsize.reshape(-1, LANES))
    (early_here,) = serve(*lookup, asked_here, 0, [early], True)
    needed = jnp.max(asked_here[:, 0] // HIGH) + 1
    early_rows = exchange(early_here)
    queries, columns, score_cols = prep(
        candidates, query_proj, score_proj.reshape(1, -1), ranks, early_here
    )
    weights = (
        key_proj.T,
        value_proj,
        out_proj,
        mlp_first,
        bias_first.reshape(1, -1),
        mlp_second,
        bias_second.reshape(1, -1),
        score_cols,
    )
    (late_here,) = serve(*lookup, score_cols, cuts[1], [cuts[2] - cuts[1]], False)

    table = jnp.zeros((scorers * span_live // LANES, LANES), jnp.float32)
    scalars = (valid_count, cand_count, span)
    shared = (scalars, (candidates, queries, columns, ranks, candidate_row))
    late_rows = exchange(late_here)
    last_rows = lax.cond(
        needed > cuts[2],
        lambda: exchange(serve(*lookup, late_rows, cuts[2], [cuts[3] - cuts[2]], False)[0]),
        lambda: jnp.zeros((devices, cuts[3] - cuts[2], width), jnp.bfloat16),
    )
    zeros = table
    table, flag_early = score(*shared, (early_rows,), weights, zeros, cuts[0:2])
    arrived = (early_rows, late_rows)
    table, flag_late = score(*shared, arrived, weights, table, cuts[1:3])
    arrived = (*arrived, last_rows)
    used = jnp.max(span[requests:]) + 1
    table = lax.cond(
        (flag_early[0] + flag_late[0] > 0) | (used >= cuts[2]),
        lambda: score(*shared, arrived, weights, zeros, (0, cuts[3]), exact=True)[0],
        lambda: table,
    )
    parts = lax.all_to_all(
        table.reshape(scorers, span_live // LANES, LANES),
        "scorer",
        split_axis=0,
        concat_axis=0,
        tiled=True,
    )
    return jnp.sum(parts, axis=0).reshape(span_live)


def solution(mesh):
    rows = P(("store", "scorer"))
    in_specs = (
        P(("store", "scorer"), None),
        rows,
        P(),
        P(("store", "scorer"), None),
        rows,
        P(("store", "scorer"), None, None),
        rows,
        P(("store", "scorer"), None),
    ) + (P(),) * 9
    return jax.shard_map(
        on_device, mesh=mesh, in_specs=in_specs, out_specs=rows, check_vma=False
    )
```

```python
import functools
import math

import jax
import jax.numpy as jnp
from jax import lax
from jax.experimental import pallas as pl
from jax.experimental.pallas import tpu as pltpu
from jax.sharding import PartitionSpec as P

HEADS = 4
LANES = 128
BLOCK = 16
DEAD = -1e30
HIGH = 65536
OFFSET_PIECES = 3
ROWS_AT_ONCE = 64
SUM_LEAST = 2.0**-100
SUM_MOST = 2.0**100
VMEM_LIMIT = 40 * 1024 * 1024


def dot(a, b):
    return jnp.dot(a, b, preferred_element_type=jnp.float32)


def dot_nt(a, b):
    return lax.dot_general(a, b, (((1,), (1,)), ((), ())), preferred_element_type=jnp.float32)


def hot(mask):
    return jnp.where(mask, 1.0, 0.0).astype(jnp.bfloat16)


def iota(shape, axis):
    return lax.broadcasted_iota(jnp.int32, shape, axis)


def whole(memory_space=pltpu.VMEM):
    return pl.BlockSpec(memory_space=memory_space)


def look_up(table_t, index, pieces):
    highs = table_t.shape[1]
    count = index.shape[1]
    rows = dot(table_t, hot(iota((highs, count), 0) == (index >> 7)))
    mine = iota((LANES, count), 0) == (index & (LANES - 1))
    found = jnp.zeros((1, count), jnp.float32)
    for piece in range(pieces):
        part = rows[piece * LANES : (piece + 1) * LANES]
        found = found + float(256**piece) * jnp.sum(
            jnp.where(mine, part, 0.0), axis=0, keepdims=True
        )
    return found


def ask_kernel(
    valid_ref, count_ref, ids_ref, home_ref, asked_ref, rank_ref, span_ref, table_ref, *, rows_dev
):
    requests, slots = ids_ref.shape
    devices, per_pair = asked_ref.shape
    pieces = table_ref.shape[0] // LANES
    for piece in range(pieces):
        part = (home_ref[...] >> (8 * piece)) & 255
        table_ref[piece * LANES : (piece + 1) * LANES, :] = jnp.transpose(
            part.astype(jnp.float32)
        ).astype(jnp.bfloat16)
    table = table_ref[...]
    upto = hot(iota((slots, slots), 0) <= iota((slots, slots), 1))
    carry = jnp.zeros((devices, 1), jnp.float32)
    asked = jnp.zeros((devices, 2 * per_pair), jnp.float32)
    for r in range(requests):
        row = look_up(table, ids_ref[r : r + 1, :], pieces).astype(jnp.int32)
        dev = row // rows_dev
        local = row - dev * rows_dev
        live = iota((1, slots), 1) < jnp.where(count_ref[r] > 0, valid_ref[r], 0)
        dest = jnp.where((iota((devices, slots), 0) == dev) & live, 1.0, 0.0)
        running = dot(dest.astype(jnp.bfloat16), upto) + carry
        carry = running[:, slots - 1 : slots]
        rank_f = jnp.sum(dest * running, axis=0, keepdims=True) - 1.0
        rank = rank_f.astype(jnp.int32)
        at_rank = iota((per_pair, slots), 0) == rank
        local_f = local.astype(jnp.float32)
        high_f = (local >> 8).astype(jnp.float32)
        low_f = local_f - 256.0 * high_f
        values = jnp.concatenate(
            [jnp.where(at_rank, low_f, 0.0), jnp.where(at_rank, high_f, 0.0)], axis=0
        )
        asked = asked + dot_nt(dest.astype(jnp.bfloat16), values.astype(jnp.bfloat16))
        rank_ref[r : r + 1, :] = jnp.where(live, dev * LANES + rank, -1)
        span_ref[r] = jnp.min(jnp.where(live, rank_f, 1e9)).astype(jnp.int32)
        span_ref[requests + r] = jnp.max(rank_f).astype(jnp.int32)
    most = jnp.max(carry, axis=0, keepdims=True)
    asked = asked[:, :per_pair] + 256.0 * asked[:, per_pair:] + HIGH * most
    asked_ref[...] = asked.astype(jnp.int32)


def ask(valid_count, cand_count, cluster_ids, home_table, devices, per_pair, rows_dev):
    requests, slots = cluster_ids.shape
    highs = home_table.shape[0]
    pieces = -(-(highs * LANES - 1).bit_length() // 8)
    return pl.pallas_call(
        functools.partial(ask_kernel, rows_dev=rows_dev),
        in_specs=[whole(pltpu.SMEM), whole(pltpu.SMEM), whole(), whole()],
        out_specs=[whole(), whole(), whole(pltpu.SMEM)],
        out_shape=[
            jax.ShapeDtypeStruct((devices, per_pair), jnp.int32),
            jax.ShapeDtypeStruct((requests, slots), jnp.int32),
            jax.ShapeDtypeStruct((2 * requests,), jnp.int32),
        ],
        scratch_shapes=[pltpu.VMEM((pieces * LANES, highs), jnp.bfloat16)],
        compiler_params=pltpu.CompilerParams(vmem_limit_bytes=VMEM_LIMIT),
        cost_estimate=pl.CostEstimate(
            flops=4_000_000_000, bytes_accessed=1_000_000, transcendentals=0
        ),
        name="ask",
    )(valid_count, cand_count, cluster_ids, home_table)


def serve_kernel(asked_ref, store_ref, size_ref, after_ref, *refs, first, sized):
    del after_ref
    out_refs, column_ref = refs[:-1], refs[-1]
    devices, per_pair = asked_ref.shape
    rows_dev, width = store_ref.shape
    places = max(out_ref.shape[1] for out_ref in out_refs)
    asked = asked_ref[...] & (HIGH - 1)
    column_ref[...] = jnp.zeros(column_ref.shape, jnp.int32)
    column_ref[1 : per_pair + 1, :] = jnp.transpose(asked.astype(jnp.float32)).astype(jnp.int32)
    group = math.gcd(devices, 1 << (384 // places).bit_length() - 1)
    store = store_ref[...]
    lanes = iota((places, rows_dev), 1)
    if sized:
        size_t = jnp.transpose(size_ref[...].astype(jnp.float32)).astype(jnp.bfloat16)
    for start in range(0, devices, group):
        picks = []
        for d in range(start, start + group):
            column = column_ref[first : first + places, d : d + 1]
            picks.append(hot(column == lanes))
        found = dot(jnp.concatenate(picks, axis=0), store).reshape(group, places, width)
        if sized:
            asked_of = [asked[d : d + 1, :] for d in range(start, start + group)]
            sizes = look_up(size_t, jnp.concatenate(asked_of, axis=1), 1)
            rest = jnp.zeros((1, width - per_pair), jnp.float32)
            for g in range(group):
                mine = sizes[:, g * per_pair : (g + 1) * per_pair]
                mine = jnp.concatenate([mine, rest], axis=1)
                top = jnp.where(iota((places, width), 0) == 0, mine, found[g])
                out_refs[0][start + g] = top.astype(jnp.bfloat16)
        else:
            found = found.astype(jnp.bfloat16)
            for out_ref in out_refs:
                out_ref[start : start + group] = found[:, : out_ref.shape[1], :]


def serve(asked_here, store_rows, size_table, after, first, place_counts, sized):
    devices, per_pair = asked_here.shape
    rows_dev, width = store_rows.shape
    places = max(place_counts)
    column_rows = max(first + places, -(-(per_pair + 1) // BLOCK) * BLOCK)
    return pl.pallas_call(
        functools.partial(serve_kernel, first=first, sized=sized),
        in_specs=[whole(), whole(), whole(), whole(pl.ANY)],
        out_specs=[whole() for _ in place_counts],
        out_shape=[
            jax.ShapeDtypeStruct((devices, count, width), jnp.bfloat16) for count in place_counts
        ],
        scratch_shapes=[pltpu.VMEM((column_rows, devices), jnp.int32)],
        compiler_params=pltpu.CompilerParams(vmem_limit_bytes=VMEM_LIMIT),
        cost_estimate=pl.CostEstimate(
            flops=2 * devices * places * rows_dev * width,
            bytes_accessed=2 * (rows_dev + devices * sum(place_counts)) * width,
            transcendentals=0,
        ),
        name="serve",
    )(asked_here, store_rows, size_table, after)


def column_of(row):
    return jnp.transpose(jnp.broadcast_to(row, (LANES, row.shape[1])))


def row_of(ref, r, columns):
    part = ref[:, columns]
    mine = jnp.where(iota(part.shape, 0) == r, part.astype(jnp.float32), 0.0)
    return jnp.sum(mine, axis=0, keepdims=True).astype(jnp.int32)


def prep_kernel(cand_ref, query_ref, score_ref, rank_ref, after_ref, *out_refs):
    queries_ref, place_ref, score_cols_ref = out_refs
    devices = after_ref.shape[0]
    cands, width = cand_ref.shape[1:]
    size = width // HEADS
    lane = iota((cands, LANES), 1)
    score = jnp.broadcast_to(score_ref[...].astype(jnp.float32), (LANES, score_ref.shape[1]))
    score_cols_ref[...] = jnp.transpose(score).astype(jnp.bfloat16)

    def one_request(r, carry):
        queries = dot(cand_ref[r], query_ref[...])
        for h in range(HEADS):
            pair = queries[:, h // 2 * LANES : (h // 2 + 1) * LANES]
            own = lane // size == h % 2
            picks = jnp.where(lane % size < OFFSET_PIECES, 1.0, 0.0)
            queries_ref[r, h] = jnp.where(own, pair, picks).astype(jnp.bfloat16)
        spot = row_of(rank_ref, r, slice(None))
        at = (spot & (LANES - 1)) + 1
        place = (at // BLOCK) * (devices * BLOCK) + (spot // LANES) * BLOCK + at % BLOCK
        place_ref[r] = column_of(jnp.where(spot >= 0, place, -1))
        return carry

    lax.fori_loop(0, cand_ref.shape[0], one_request, 0)


def prep(candidates, query_proj, score_proj, ranks, after):
    requests, cands, width = candidates.shape
    return pl.pallas_call(
        prep_kernel,
        in_specs=[whole() for _ in range(4)] + [whole(pl.ANY)],
        out_specs=[whole() for _ in range(3)],
        out_shape=[
            jax.ShapeDtypeStruct((requests, HEADS, cands, LANES), jnp.bfloat16),
            jax.ShapeDtypeStruct((*ranks.shape, LANES), jnp.int32),
            jax.ShapeDtypeStruct((score_proj.shape[1], LANES), jnp.bfloat16),
        ],
        compiler_params=pltpu.CompilerParams(vmem_limit_bytes=VMEM_LIMIT),
        cost_estimate=pl.CostEstimate(
            flops=2 * requests * cands * width * width,
            bytes_accessed=10 * requests * cands * width,
            transcendentals=0,
        ),
        name="prep",
    )(candidates, query_proj, score_proj, ranks, after)


def score_kernel(*refs, bases, from_place, to_place, exact):
    valid_ref, count_ref, span_ref = refs[:3]
    cand_all, queries_all, place_all, rank_ref, target_ref = refs[3:8]
    arrived_all = refs[8 : 8 + len(bases)]
    (
        key_ref,
        value_ref,
        out_proj_ref,
        first_ref,
        bias_first_ref,
        second_ref,
        bias_second_ref,
        score_ref,
        before_ref,
        table_ref,
        flag_ref,
        rows_ref,
        keys_ref,
        values_ref,
        context_ref,
        least_ref,
        most_ref,
        size_ref,
        cand_ref,
        queries_ref,
        place_ref,
        arrived_sems,
        request_sems,
        *arrived_refs,
    ) = refs[8 + len(bases) :]
    requests, slots = rank_ref.shape
    devices = arrived_refs[0].shape[0]
    cands, width = cand_ref.shape[1:]
    head_size = width // HEADS
    cand_part = math.gcd(cands, 256)
    highs = table_ref.shape[0]
    scale = math.sqrt(head_size)
    to_log2 = math.log2(math.e) / scale
    sizes_done = [slots] if exact else range(slots // 2, slots + 1, LANES)
    fetched = ((place_all, place_ref), (queries_all, queries_ref), (cand_all, cand_ref))
    own_rows = [slice(h % 2 * head_size, (h % 2 + 1) * head_size) for h in range(HEADS)]
    other_rows = [slice((1 - h % 2) * head_size, (2 - h % 2) * head_size) for h in range(HEADS)]

    def is_mine(r):
        last_place = span_ref[requests + r] + 1
        return (count_ref[r] > 0) & (last_place >= from_place) & (last_place < to_place)

    def copies_of(r):
        return [
            pltpu.make_async_copy(source.at[r], target.at[r], request_sems.at[i, r])
            for i, (source, target) in enumerate(fetched)
        ]

    arrivals = [
        pltpu.make_async_copy(source, target, arrived_sems.at[i])
        for i, (source, target) in enumerate(zip(arrived_all, arrived_refs))
    ]
    for copy in arrivals:
        copy.start()
    for r in range(requests):

        @pl.when(is_mine(r))
        def _():
            for copy in copies_of(r):
                copy.start()

    keys_ref[...] = jnp.zeros(keys_ref.shape, jnp.bfloat16)
    values_ref[...] = jnp.zeros(values_ref.shape, jnp.bfloat16)
    for copy in arrivals:
        copy.wait()
    heads_of = arrived_refs[0][:, :BLOCK, :LANES].astype(jnp.float32)
    at_top = iota(heads_of.shape, 1) == 0
    sizes = jnp.sum(jnp.where(at_top, heads_of, 0.0), axis=1)
    size_ref[...] = jnp.transpose(sizes).astype(jnp.bfloat16)

    def select(r, n, arrived_ref, base):
        block_rows = devices * BLOCK
        blocks = arrived_ref.shape[1] // BLOCK
        at_once = min(2, blocks)
        low_block = jnp.clip((span_ref[r] + 1) // BLOCK - base, 0, blocks)
        high_block = jnp.clip((span_ref[requests + r] + 1) // BLOCK + 1 - base, 0, blocks)

        def step(i, carry):
            wanted = low_block + i * at_once
            j = jnp.minimum(wanted, blocks - at_once)
            place = place_ref[r, :n, :]
            rel = jnp.where(place >= (wanted + base) * block_rows, place, -1)
            rel = rel - (j + base) * block_rows
            lanes = iota((n, LANES), 1)
            found = []
            for b in range(at_once):
                start = pl.multiple_of((j + b) * BLOCK, BLOCK)
                block = arrived_ref[:, pl.ds(start, BLOCK), :].reshape(block_rows, width)
                firsts = range(b * block_rows, (b + 1) * block_rows, LANES)
                picks = [hot(rel == lanes + first) for first in firsts]
                found.append(dot(jnp.concatenate(picks, axis=1), block))
            rows_ref[:n, :] += sum(found)
            return carry

        lax.fori_loop(0, (high_block - low_block + at_once - 1) // at_once, step, 0)

    def load(r, n):
        rows_ref[:n, :] = jnp.zeros((n, width), jnp.float32)
        for arrived_ref, base in zip(arrived_refs, bases):
            select(r, n, arrived_ref, base)
        spot = row_of(rank_ref, r, slice(0, n))
        size = look_up(size_ref[...], spot, 1)
        largest = jnp.max(jnp.where(spot >= 0, size, DEAD), axis=1, keepdims=True)
        left = jnp.where(spot >= 0, (size - largest) * scale, DEAD)
        pieces = jnp.zeros((head_size, n), jnp.float32)
        for row in range(OFFSET_PIECES):
            piece = left.astype(jnp.bfloat16).astype(jnp.float32)
            left = left - piece
            pieces = jnp.where(iota((head_size, n), 0) == row, piece, pieces)
        pieces = pieces.astype(jnp.bfloat16)
        rows = rows_ref[:n, :].astype(jnp.bfloat16)
        keys = dot_nt(key_ref[...], rows).astype(jnp.bfloat16)
        values = dot(rows, value_ref[...])
        own = iota((n, LANES), 1) // head_size
        for h in range(HEADS):
            keys_ref[h, own_rows[h], :n] = keys[h * head_size : (h + 1) * head_size]
            keys_ref[h, other_rows[h], :n] = pieces
            if n < slots:
                rest = (head_size, slots - n)
                dead = jnp.where(iota(rest, 0) == 0, DEAD, 0.0).astype(jnp.bfloat16)
                keys_ref[h, other_rows[h], n:] = dead
            pair = values[:, h // 2 * LANES : (h // 2 + 1) * LANES]
            first = h % 2 * n
            values_ref[h // 2, first : first + n, :] = jnp.where(own == h % 2, pair, 0.0).astype(
                jnp.bfloat16
            )

    def attend(r, n, slot):
        least = least_ref[...]
        most = most_ref[...]
        for pair in range(HEADS // 2):
            probs = []
            for h in (2 * pair, 2 * pair + 1):
                logits = dot(queries_ref[r, h], keys_ref[h, :, :n])
                of_head = []
                for first in range(0, cands, ROWS_AT_ONCE):
                    weights = jnp.exp2(logits[first : first + ROWS_AT_ONCE] * to_log2)
                    total = jnp.sum(weights, axis=1, keepdims=True)
                    least = jnp.minimum(least, total)
                    most = jnp.maximum(most, total)
                    of_head.append((weights * (1.0 / total)).astype(jnp.bfloat16))
                probs.append(jnp.concatenate(of_head, axis=0))
            context = dot(jnp.concatenate(probs, axis=1), values_ref[pair, : 2 * n, :])
            context_ref[slot, :, pair * LANES : (pair + 1) * LANES] = context.astype(jnp.bfloat16)
        least_ref[...] = least
        most_ref[...] = most

    def attend_exactly(r, slot):
        def part(c, carry):
            rows = pl.ds(pl.multiple_of(c * cand_part, cand_part), cand_part)
            for pair in range(HEADS // 2):
                probs = []
                for h in (2 * pair, 2 * pair + 1):
                    logits = dot(queries_ref[r, h, rows, :], keys_ref[h])
                    top = jnp.max(logits, axis=1, keepdims=True)
                    weights = jnp.exp2((logits - top) * to_log2)
                    total = jnp.sum(weights, axis=1, keepdims=True)
                    probs.append((weights * (1.0 / total)).astype(jnp.bfloat16))
                context = dot(jnp.concatenate(probs, axis=1), values_ref[pair])
                columns = slice(pair * LANES, (pair + 1) * LANES)
                context_ref[slot, rows, columns] = context.astype(jnp.bfloat16)
            return carry

        lax.fori_loop(0, cands // cand_part, part, 0)

    def rate(last, slot):
        r = jnp.maximum(last, 0)
        attended = dot(context_ref[slot], out_proj_ref[...]).astype(jnp.bfloat16)
        hidden = (
            dot(cand_ref[r], first_ref[:width, :])
            + dot(attended, first_ref[width:, :])
            + bias_first_ref[...]
        )
        hidden = jnp.maximum(hidden, 0.0).astype(jnp.bfloat16)
        hidden = dot(hidden, second_ref[...]) + bias_second_ref[...]
        hidden = jnp.maximum(hidden, 0.0).astype(jnp.bfloat16)
        scores = jnp.transpose(dot(hidden, score_ref[...]))[:1]
        target = row_of(target_ref, r, slice(None))
        counted = iota((1, cands), 1) < jnp.where(last >= 0, count_ref[r], 0)
        high_hot = hot((iota((highs, cands), 0) == (target >> 7)) & counted)
        at_low = iota((LANES, cands), 0) == (target & (LANES - 1))
        left = jnp.where(counted, scores, 0.0)
        pieces = []
        for _ in range(3):
            piece = left.astype(jnp.bfloat16).astype(jnp.float32)
            left = left - piece
            pieces.append(jnp.where(at_low, piece, 0.0).astype(jnp.bfloat16))
        found = dot_nt(high_hot, jnp.concatenate(pieces, axis=0))
        table_ref[...] += sum(found[:, i * LANES : (i + 1) * LANES] for i in range(3))

    def one_request(r, carry):
        last, slot = carry
        valid = valid_ref[r]
        mine = is_mine(r)

        @pl.when(mine)
        def _():
            for copy in copies_of(r):
                copy.wait()
            fewer = 0
            for n in sizes_done:

                @pl.when((valid > fewer) & (valid <= n))
                def _():
                    load(r, n)
                    if exact:
                        attend_exactly(r, slot)
                        rate(r, slot)
                    else:
                        rate(last, slot)
                        attend(r, n, 1 - slot)

                fewer = n

        return jnp.where(mine, r, last), jnp.where(mine, 1 - slot, slot)

    table_ref[...] = before_ref[...]
    least_ref[...] = jnp.ones(least_ref.shape, jnp.float32)
    most_ref[...] = jnp.ones(most_ref.shape, jnp.float32)
    context_ref[...] = jnp.zeros(context_ref.shape, jnp.bfloat16)
    last, slot = lax.fori_loop(0, requests, one_request, (jnp.int32(-1), jnp.int32(0)))
    if not exact:

        @pl.when(last >= 0)
        def _():
            rate(last, slot)

    in_range = (jnp.min(least_ref[...]) >= SUM_LEAST) & (jnp.max(most_ref[...]) <= SUM_MOST)
    flag_ref[0] = jnp.where(in_range, 0, 1)


def score(scalars, operands, arrived, weights, before, places, exact=False):
    candidates, queries, columns, ranks, _ = operands
    cands, width = candidates.shape[1:]
    slots = ranks.shape[1]
    devices = arrived[0].shape[0]
    bases = []
    for rows in arrived:
        bases.append(bases[-1] + arrived[len(bases) - 1].shape[1] // BLOCK if bases else 0)
    operands = [*operands, *arrived, *weights, before]
    return pl.pallas_call(
        functools.partial(
            score_kernel,
            bases=tuple(bases),
            from_place=places[0],
            to_place=places[1],
            exact=exact,
        ),
        in_specs=[whole(pltpu.SMEM)] * 3
        + [whole(pl.ANY)] * 3
        + [whole()] * 2
        + [whole(pl.ANY)] * len(arrived)
        + [whole() for _ in (*weights, before)],
        out_specs=[whole(), whole(pltpu.SMEM)],
        scratch_shapes=[
            pltpu.VMEM((slots, width), jnp.float32),
            pltpu.VMEM((HEADS, LANES, slots), jnp.bfloat16),
            pltpu.VMEM((HEADS // 2, 2 * slots, LANES), jnp.bfloat16),
            pltpu.VMEM((2, cands, width), jnp.bfloat16),
            pltpu.VMEM((ROWS_AT_ONCE, 1), jnp.float32),
            pltpu.VMEM((ROWS_AT_ONCE, 1), jnp.float32),
            pltpu.VMEM((LANES, devices), jnp.bfloat16),
            pltpu.VMEM(candidates.shape, candidates.dtype),
            pltpu.VMEM(queries.shape, queries.dtype),
            pltpu.VMEM(columns.shape, columns.dtype),
            pltpu.SemaphoreType.DMA((len(arrived),)),
            pltpu.SemaphoreType.DMA((3, ranks.shape[0])),
            *(pltpu.VMEM(rows.shape, rows.dtype) for rows in arrived),
        ],
        out_shape=[
            jax.ShapeDtypeStruct(before.shape, jnp.float32),
            jax.ShapeDtypeStruct((1,), jnp.int32),
        ],
        compiler_params=pltpu.CompilerParams(vmem_limit_bytes=VMEM_LIMIT),
        cost_estimate=pl.CostEstimate(
            flops=10_000_000_000, bytes_accessed=5_000_000, transcendentals=4_000_000
        ),
        name="score",
    )(*scalars, *operands)


def on_device(
    store_rows,
    cluster_logsize,
    cluster_home,
    cluster_ids,
    valid_count,
    candidates,
    cand_count,
    candidate_row,
    query_proj,
    key_proj,
    value_proj,
    out_proj,
    mlp_first,
    bias_first,
    mlp_second,
    bias_second,
    score_proj,
):
    axes = ("store", "scorer")
    devices = lax.axis_size(axes)
    scorers = lax.axis_size("scorer")
    requests, slots = cluster_ids.shape
    rows_dev, width = store_rows.shape
    cands = candidates.shape[1]
    per_pair = requests * slots // devices
    span_live = requests * cands // 2

    exchange = functools.partial(
        lax.all_to_all, axis_name=axes, split_axis=0, concat_axis=0, tiled=True
    )
    asked, ranks, span = ask(
        valid_count,
        cand_count,
        cluster_ids,
        cluster_home.reshape(-1, LANES),
        devices,
        per_pair,
        rows_dev,
    )
    asked_here = exchange(asked)
    in_blocks = lambda places: -(-places // BLOCK) * BLOCK
    early = in_blocks(per_pair // 2)
    cuts = (0, early, in_blocks(7 * per_pair // 8), in_blocks(per_pair + 1))
    lookup = (asked_here, store_rows, cluster_logsize.reshape(-1, LANES))
    (early_here,) = serve(*lookup, asked_here, 0, [early], True)
    needed = jnp.max(asked_here[:, 0] // HIGH) + 1
    early_rows = exchange(early_here)
    queries, columns, score_cols = prep(
        candidates, query_proj, score_proj.reshape(1, -1), ranks, early_here
    )
    weights = (
        key_proj.T,
        value_proj,
        out_proj,
        mlp_first,
        bias_first.reshape(1, -1),
        mlp_second,
        bias_second.reshape(1, -1),
        score_cols,
    )
    (late_here,) = serve(*lookup, score_cols, cuts[1], [cuts[2] - cuts[1]], False)

    table = jnp.zeros((scorers * span_live // LANES, LANES), jnp.float32)
    scalars = (valid_count, cand_count, span)
    shared = (scalars, (candidates, queries, columns, ranks, candidate_row))
    late_here, early_rows = lax.optimization_barrier((late_here, early_rows))
    late_rows = exchange(late_here)
    last_rows = lax.cond(
        needed > cuts[2],
        lambda: exchange(serve(*lookup, late_rows, cuts[2], [cuts[3] - cuts[2]], False)[0]),
        lambda: jnp.zeros((devices, cuts[3] - cuts[2], width), jnp.bfloat16),
    )
    zeros = table
    table, flag_early = score(*shared, (early_rows,), weights, zeros, cuts[0:2])
    arrived = (early_rows, late_rows)
    table, flag_late = score(*shared, arrived, weights, table, cuts[1:3])
    arrived = (*arrived, last_rows)
    used = jnp.max(span[requests:]) + 1
    table = lax.cond(
        (flag_early[0] + flag_late[0] > 0) | (used >= cuts[2]),
        lambda: score(*shared, arrived, weights, zeros, (0, cuts[3]), exact=True)[0],
        lambda: table,
    )
    parts = lax.all_to_all(
        table.reshape(scorers, span_live // LANES, LANES),
        "scorer",
        split_axis=0,
        concat_axis=0,
        tiled=True,
    )
    return jnp.sum(parts, axis=0).reshape(span_live)


def solution(mesh):
    rows = P(("store", "scorer"))
    in_specs = (
        P(("store", "scorer"), None),
        rows,
        P(),
        P(("store", "scorer"), None),
        rows,
        P(("store", "scorer"), None, None),
        rows,
        P(("store", "scorer"), None),
    ) + (P(),) * 9
    return jax.shard_map(
        on_device, mesh=mesh, in_specs=in_specs, out_specs=rows, check_vma=False
    )
```

```python
import functools
import math

import jax
import jax.numpy as jnp
from jax import lax
from jax.experimental import pallas as pl
from jax.experimental.pallas import tpu as pltpu
from jax.sharding import PartitionSpec as P

HEADS = 4
LANES = 128
BLOCK = 16
DEAD = -1e30
HIGH = 65536
OFFSET_PIECES = 3
ROWS_AT_ONCE = 64
SUM_LEAST = 2.0**-100
SUM_MOST = 2.0**100
VMEM_LIMIT = 40 * 1024 * 1024


def dot(a, b):
    return jnp.dot(a, b, preferred_element_type=jnp.float32)


def dot_nt(a, b):
    return lax.dot_general(a, b, (((1,), (1,)), ((), ())), preferred_element_type=jnp.float32)


def hot(mask):
    return jnp.where(mask, 1.0, 0.0).astype(jnp.bfloat16)


def iota(shape, axis):
    return lax.broadcasted_iota(jnp.int32, shape, axis)


def whole(memory_space=pltpu.VMEM):
    return pl.BlockSpec(memory_space=memory_space)


def look_up(table_t, index, pieces):
    highs = table_t.shape[1]
    count = index.shape[1]
    rows = dot(table_t, hot(iota((highs, count), 0) == (index >> 7)))
    mine = iota((LANES, count), 0) == (index & (LANES - 1))
    found = jnp.zeros((1, count), jnp.float32)
    for piece in range(pieces):
        part = rows[piece * LANES : (piece + 1) * LANES]
        found = found + float(256**piece) * jnp.sum(
            jnp.where(mine, part, 0.0), axis=0, keepdims=True
        )
    return found


def ask_kernel(
    valid_ref, count_ref, ids_ref, home_ref, asked_ref, rank_ref, span_ref, table_ref, *, rows_dev
):
    requests, slots = ids_ref.shape
    devices, per_pair = asked_ref.shape
    pieces = table_ref.shape[0] // LANES
    for piece in range(pieces):
        part = (home_ref[...] >> (8 * piece)) & 255
        table_ref[piece * LANES : (piece + 1) * LANES, :] = jnp.transpose(
            part.astype(jnp.float32)
        ).astype(jnp.bfloat16)
    table = table_ref[...]
    upto = hot(iota((slots, slots), 0) <= iota((slots, slots), 1))
    carry = jnp.zeros((devices, 1), jnp.float32)
    asked = jnp.zeros((devices, 2 * per_pair), jnp.float32)
    for r in range(requests):
        row = look_up(table, ids_ref[r : r + 1, :], pieces).astype(jnp.int32)
        dev = row // rows_dev
        local = row - dev * rows_dev
        live = iota((1, slots), 1) < jnp.where(count_ref[r] > 0, valid_ref[r], 0)
        dest = jnp.where((iota((devices, slots), 0) == dev) & live, 1.0, 0.0)
        running = dot(dest.astype(jnp.bfloat16), upto) + carry
        carry = running[:, slots - 1 : slots]
        rank_f = jnp.sum(dest * running, axis=0, keepdims=True) - 1.0
        rank = rank_f.astype(jnp.int32)
        at_rank = iota((per_pair, slots), 0) == rank
        local_f = local.astype(jnp.float32)
        high_f = (local >> 8).astype(jnp.float32)
        low_f = local_f - 256.0 * high_f
        values = jnp.concatenate(
            [jnp.where(at_rank, low_f, 0.0), jnp.where(at_rank, high_f, 0.0)], axis=0
        )
        asked = asked + dot_nt(dest.astype(jnp.bfloat16), values.astype(jnp.bfloat16))
        rank_ref[r : r + 1, :] = jnp.where(live, dev * LANES + rank, -1)
        span_ref[r] = jnp.min(jnp.where(live, rank_f, 1e9)).astype(jnp.int32)
        span_ref[requests + r] = jnp.max(rank_f).astype(jnp.int32)
    most = jnp.max(carry, axis=0, keepdims=True)
    asked = asked[:, :per_pair] + 256.0 * asked[:, per_pair:] + HIGH * most
    asked_ref[...] = asked.astype(jnp.int32)


def ask(valid_count, cand_count, cluster_ids, home_table, devices, per_pair, rows_dev):
    requests, slots = cluster_ids.shape
    highs = home_table.shape[0]
    pieces = -(-(highs * LANES - 1).bit_length() // 8)
    return pl.pallas_call(
        functools.partial(ask_kernel, rows_dev=rows_dev),
        in_specs=[whole(pltpu.SMEM), whole(pltpu.SMEM), whole(), whole()],
        out_specs=[whole(), whole(), whole(pltpu.SMEM)],
        out_shape=[
            jax.ShapeDtypeStruct((devices, per_pair), jnp.int32),
            jax.ShapeDtypeStruct((requests, slots), jnp.int32),
            jax.ShapeDtypeStruct((2 * requests,), jnp.int32),
        ],
        scratch_shapes=[pltpu.VMEM((pieces * LANES, highs), jnp.bfloat16)],
        compiler_params=pltpu.CompilerParams(vmem_limit_bytes=VMEM_LIMIT),
        cost_estimate=pl.CostEstimate(
            flops=4_000_000_000, bytes_accessed=1_000_000, transcendentals=0
        ),
        name="ask",
    )(valid_count, cand_count, cluster_ids, home_table)


def serve_kernel(asked_ref, store_ref, size_ref, after_ref, *refs, first, sized):
    del after_ref
    *out_refs, most_ref, column_ref = refs
    devices, per_pair = asked_ref.shape
    rows_dev, width = store_ref.shape
    places = max(out_ref.shape[1] for out_ref in out_refs)
    most_ref[0] = jnp.max((asked_ref[...] // HIGH).astype(jnp.float32)).astype(jnp.int32)
    asked = asked_ref[...] & (HIGH - 1)
    column_ref[...] = jnp.zeros(column_ref.shape, jnp.int32)
    column_ref[1 : per_pair + 1, :] = jnp.transpose(asked.astype(jnp.float32)).astype(jnp.int32)
    group = math.gcd(devices, 1 << (384 // places).bit_length() - 1)
    store = store_ref[...]
    lanes = iota((places, rows_dev), 1)
    if sized:
        size_t = jnp.transpose(size_ref[...].astype(jnp.float32)).astype(jnp.bfloat16)
    for start in range(0, devices, group):
        picks = []
        for d in range(start, start + group):
            column = column_ref[first : first + places, d : d + 1]
            picks.append(hot(column == lanes))
        found = dot(jnp.concatenate(picks, axis=0), store).reshape(group, places, width)
        if sized:
            asked_of = [asked[d : d + 1, :] for d in range(start, start + group)]
            sizes = look_up(size_t, jnp.concatenate(asked_of, axis=1), 1)
            rest = jnp.zeros((1, width - per_pair), jnp.float32)
            for g in range(group):
                mine = sizes[:, g * per_pair : (g + 1) * per_pair]
                mine = jnp.concatenate([mine, rest], axis=1)
                top = jnp.where(iota((places, width), 0) == 0, mine, found[g])
                out_refs[0][start + g] = top.astype(jnp.bfloat16)
        else:
            found = found.astype(jnp.bfloat16)
            for out_ref in out_refs:
                out_ref[start : start + group] = found[:, : out_ref.shape[1], :]


def serve(asked_here, store_rows, size_table, after, first, place_counts, sized):
    devices, per_pair = asked_here.shape
    rows_dev, width = store_rows.shape
    places = max(place_counts)
    column_rows = max(first + places, -(-(per_pair + 1) // BLOCK) * BLOCK)
    return pl.pallas_call(
        functools.partial(serve_kernel, first=first, sized=sized),
        in_specs=[whole(), whole(), whole(), whole(pl.ANY)],
        out_specs=[whole() for _ in place_counts] + [whole(pltpu.SMEM)],
        out_shape=[
            jax.ShapeDtypeStruct((devices, count, width), jnp.bfloat16) for count in place_counts
        ]
        + [jax.ShapeDtypeStruct((1,), jnp.int32)],
        scratch_shapes=[pltpu.VMEM((column_rows, devices), jnp.int32)],
        compiler_params=pltpu.CompilerParams(vmem_limit_bytes=VMEM_LIMIT),
        cost_estimate=pl.CostEstimate(
            flops=2 * devices * places * rows_dev * width,
            bytes_accessed=2 * (rows_dev + devices * sum(place_counts)) * width,
            transcendentals=0,
        ),
        name="serve",
    )(asked_here, store_rows, size_table, after)


def column_of(row):
    return jnp.transpose(jnp.broadcast_to(row, (LANES, row.shape[1])))


def row_of(ref, r, columns):
    part = ref[:, columns]
    mine = jnp.where(iota(part.shape, 0) == r, part.astype(jnp.float32), 0.0)
    return jnp.sum(mine, axis=0, keepdims=True).astype(jnp.int32)


def prep_kernel(
    cand_ref, query_ref, first_ref, bias_first_ref, score_ref, rank_ref, after_ref, *out_refs
):
    queries_ref, base_ref, place_ref, score_cols_ref = out_refs
    devices = after_ref.shape[0]
    cands, width = cand_ref.shape[1:]
    size = width // HEADS
    lane = iota((cands, LANES), 1)
    score = jnp.broadcast_to(score_ref[...].astype(jnp.float32), (LANES, score_ref.shape[1]))
    score_cols_ref[...] = jnp.transpose(score).astype(jnp.bfloat16)

    def one_request(r, carry):
        queries = dot(cand_ref[r], query_ref[...])
        for h in range(HEADS):
            pair = queries[:, h // 2 * LANES : (h // 2 + 1) * LANES]
            own = lane // size == h % 2
            picks = jnp.where(lane % size < OFFSET_PIECES, 1.0, 0.0)
            queries_ref[r, h] = jnp.where(own, pair, picks).astype(jnp.bfloat16)
        base_ref[r] = dot(cand_ref[r], first_ref[:width, :]) + bias_first_ref[...]
        spot = row_of(rank_ref, r, slice(None))
        at = (spot & (LANES - 1)) + 1
        place = (at // BLOCK) * (devices * BLOCK) + (spot // LANES) * BLOCK + at % BLOCK
        place_ref[r] = column_of(jnp.where(spot >= 0, place, -1))
        return carry

    lax.fori_loop(0, cand_ref.shape[0], one_request, 0)


def prep(candidates, query_proj, mlp_first, bias_first, score_proj, ranks, after):
    requests, cands, width = candidates.shape
    units = mlp_first.shape[1]
    return pl.pallas_call(
        prep_kernel,
        in_specs=[whole() for _ in range(6)] + [whole(pl.ANY)],
        out_specs=[whole() for _ in range(4)],
        out_shape=[
            jax.ShapeDtypeStruct((requests, HEADS, cands, LANES), jnp.bfloat16),
            jax.ShapeDtypeStruct((requests, cands, units), jnp.float32),
            jax.ShapeDtypeStruct((*ranks.shape, LANES), jnp.int32),
            jax.ShapeDtypeStruct((score_proj.shape[1], LANES), jnp.bfloat16),
        ],
        compiler_params=pltpu.CompilerParams(vmem_limit_bytes=VMEM_LIMIT),
        cost_estimate=pl.CostEstimate(
            flops=2 * requests * cands * width * (width + units),
            bytes_accessed=18 * requests * cands * width,
            transcendentals=0,
        ),
        name="prep",
    )(candidates, query_proj, mlp_first, bias_first, score_proj, ranks, after)


def score_kernel(*refs, bases, from_place, to_place, spare):
    valid_ref, count_ref, span_ref, before_flag_ref = refs[:4]
    base_all, queries_all, place_all, rank_ref, target_ref = refs[4:9]
    arrived_all = refs[9 : 9 + len(bases)]
    (
        key_ref,
        value_ref,
        out_proj_ref,
        first_ref,
        second_ref,
        bias_second_ref,
        score_ref,
        before_ref,
        table_ref,
        flag_ref,
        rows_ref,
        keys_ref,
        values_ref,
        context_ref,
        least_ref,
        most_ref,
        size_ref,
        base_ref,
        queries_ref,
        place_ref,
        arrived_sems,
        request_sems,
        *arrived_refs,
    ) = refs[9 + len(bases) :]
    requests, slots = rank_ref.shape
    devices = arrived_refs[0].shape[0]
    cands = base_ref.shape[1]
    width = rows_ref.shape[1]
    head_size = width // HEADS
    cand_part = math.gcd(cands, 256)
    highs = table_ref.shape[0]
    scale = math.sqrt(head_size)
    to_log2 = math.log2(math.e) / scale
    sizes_done = range(slots // 2, slots + 1, LANES)
    at_hand = len(bases) - 1 if spare else len(bases)
    fetched = ((place_all, place_ref), (queries_all, queries_ref), (base_all, base_ref))
    own_rows = [slice(h % 2 * head_size, (h % 2 + 1) * head_size) for h in range(HEADS)]
    other_rows = [slice((1 - h % 2) * head_size, (2 - h % 2) * head_size) for h in range(HEADS)]

    def is_mine(r):
        last_place = span_ref[requests + r] + 1
        return (count_ref[r] > 0) & (last_place >= from_place) & (last_place < to_place)

    def copies_of(r):
        return [
            pltpu.make_async_copy(source.at[r], target.at[r], request_sems.at[i, r])
            for i, (source, target) in enumerate(fetched)
        ]

    arrivals = [
        pltpu.make_async_copy(source, target, arrived_sems.at[i])
        for i, (source, target) in enumerate(zip(arrived_all, arrived_refs))
    ]
    for copy in arrivals[:at_hand]:
        copy.start()
    for r in range(requests):

        @pl.when(is_mine(r))
        def _():
            for copy in copies_of(r):
                copy.start()

    keys_ref[...] = jnp.zeros(keys_ref.shape, jnp.bfloat16)
    values_ref[...] = jnp.zeros(values_ref.shape, jnp.bfloat16)
    for copy in arrivals[:at_hand]:
        copy.wait()
    heads_of = arrived_refs[0][:, :BLOCK, :LANES].astype(jnp.float32)
    at_top = iota(heads_of.shape, 1) == 0
    sizes = jnp.sum(jnp.where(at_top, heads_of, 0.0), axis=1)
    size_ref[...] = jnp.transpose(sizes).astype(jnp.bfloat16)

    def select(r, n, arrived_ref, base):
        block_rows = devices * BLOCK
        blocks = arrived_ref.shape[1] // BLOCK
        at_once = min(2, blocks)
        low_block = jnp.clip((span_ref[r] + 1) // BLOCK - base, 0, blocks)
        high_block = jnp.clip((span_ref[requests + r] + 1) // BLOCK + 1 - base, 0, blocks)

        def step(i, carry):
            wanted = low_block + i * at_once
            j = jnp.minimum(wanted, blocks - at_once)
            place = place_ref[r, :n, :]
            rel = jnp.where(place >= (wanted + base) * block_rows, place, -1)
            rel = rel - (j + base) * block_rows
            lanes = iota((n, LANES), 1)
            found = []
            for b in range(at_once):
                start = pl.multiple_of((j + b) * BLOCK, BLOCK)
                block = arrived_ref[:, pl.ds(start, BLOCK), :].reshape(block_rows, width)
                firsts = range(b * block_rows, (b + 1) * block_rows, LANES)
                picks = [hot(rel == lanes + first) for first in firsts]
                found.append(dot(jnp.concatenate(picks, axis=1), block))
            rows_ref[:n, :] += sum(found)
            return carry

        lax.fori_loop(0, (high_block - low_block + at_once - 1) // at_once, step, 0)

    def load(r, n, blocks_at_hand):
        rows_ref[:n, :] = jnp.zeros((n, width), jnp.float32)
        for arrived_ref, base in list(zip(arrived_refs, bases))[:blocks_at_hand]:
            select(r, n, arrived_ref, base)
        spot = row_of(rank_ref, r, slice(0, n))
        size = look_up(size_ref[...], spot, 1)
        largest = jnp.max(jnp.where(spot >= 0, size, DEAD), axis=1, keepdims=True)
        left = jnp.where(spot >= 0, (size - largest) * scale, DEAD)
        pieces = jnp.zeros((head_size, n), jnp.float32)
        for row in range(OFFSET_PIECES):
            piece = left.astype(jnp.bfloat16).astype(jnp.float32)
            left = left - piece
            pieces = jnp.where(iota((head_size, n), 0) == row, piece, pieces)
        pieces = pieces.astype(jnp.bfloat16)
        rows = rows_ref[:n, :].astype(jnp.bfloat16)
        keys = dot_nt(key_ref[...], rows).astype(jnp.bfloat16)
        values = dot(rows, value_ref[...])
        own = iota((n, LANES), 1) // head_size
        for h in range(HEADS):
            keys_ref[h, own_rows[h], :n] = keys[h * head_size : (h + 1) * head_size]
            keys_ref[h, other_rows[h], :n] = pieces
            if n < slots:
                rest = (head_size, slots - n)
                dead = jnp.where(iota(rest, 0) == 0, DEAD, 0.0).astype(jnp.bfloat16)
                keys_ref[h, other_rows[h], n:] = dead
            pair = values[:, h // 2 * LANES : (h // 2 + 1) * LANES]
            first = h % 2 * n
            values_ref[h // 2, first : first + n, :] = jnp.where(own == h % 2, pair, 0.0).astype(
                jnp.bfloat16
            )

    def attend(r, n, slot):
        least = least_ref[...]
        most = most_ref[...]
        for pair in range(HEADS // 2):
            probs = []
            for h in (2 * pair, 2 * pair + 1):
                logits = dot(queries_ref[r, h], keys_ref[h, :, :n])
                of_head = []
                for first in range(0, cands, ROWS_AT_ONCE):
                    weights = jnp.exp2(logits[first : first + ROWS_AT_ONCE] * to_log2)
                    total = jnp.sum(weights, axis=1, keepdims=True)
                    least = jnp.minimum(least, total)
                    most = jnp.maximum(most, total)
                    of_head.append((weights * (1.0 / total)).astype(jnp.bfloat16))
                probs.append(jnp.concatenate(of_head, axis=0))
            context = dot(jnp.concatenate(probs, axis=1), values_ref[pair, : 2 * n, :])
            context_ref[slot, :, pair * LANES : (pair + 1) * LANES] = context.astype(jnp.bfloat16)
        least_ref[...] = least
        most_ref[...] = most

    def attend_exactly(r, slot):
        def part(c, carry):
            rows = pl.ds(pl.multiple_of(c * cand_part, cand_part), cand_part)
            for pair in range(HEADS // 2):
                probs = []
                for h in (2 * pair, 2 * pair + 1):
                    logits = dot(queries_ref[r, h, rows, :], keys_ref[h])
                    top = jnp.max(logits, axis=1, keepdims=True)
                    weights = jnp.exp2((logits - top) * to_log2)
                    total = jnp.sum(weights, axis=1, keepdims=True)
                    probs.append((weights * (1.0 / total)).astype(jnp.bfloat16))
                context = dot(jnp.concatenate(probs, axis=1), values_ref[pair])
                columns = slice(pair * LANES, (pair + 1) * LANES)
                context_ref[slot, rows, columns] = context.astype(jnp.bfloat16)
            return carry

        lax.fori_loop(0, cands // cand_part, part, 0)

    def rate(last, slot):
        r = jnp.maximum(last, 0)
        attended = dot(context_ref[slot], out_proj_ref[...]).astype(jnp.bfloat16)
        hidden = dot(attended, first_ref[width:, :]) + base_ref[r]
        hidden = jnp.maximum(hidden, 0.0).astype(jnp.bfloat16)
        hidden = dot(hidden, second_ref[...]) + bias_second_ref[...]
        hidden = jnp.maximum(hidden, 0.0).astype(jnp.bfloat16)
        scores = jnp.transpose(dot(hidden, score_ref[...]))[:1]
        target = row_of(target_ref, r, slice(None))
        counted = iota((1, cands), 1) < jnp.where(last >= 0, count_ref[r], 0)
        high_hot = hot((iota((highs, cands), 0) == (target >> 7)) & counted)
        at_low = iota((LANES, cands), 0) == (target & (LANES - 1))
        left = jnp.where(counted, scores, 0.0)
        pieces = []
        for _ in range(3):
            piece = left.astype(jnp.bfloat16).astype(jnp.float32)
            left = left - piece
            pieces.append(jnp.where(at_low, piece, 0.0).astype(jnp.bfloat16))
        found = dot_nt(high_hot, jnp.concatenate(pieces, axis=0))
        table_ref[...] += sum(found[:, i * LANES : (i + 1) * LANES] for i in range(3))

    def one_request(r, carry):
        last, slot = carry
        valid = valid_ref[r]
        mine = is_mine(r)

        @pl.when(mine)
        def _():
            for copy in copies_of(r):
                copy.wait()
            fewer = 0
            for n in sizes_done:

                @pl.when((valid > fewer) & (valid <= n))
                def _():
                    load(r, n, at_hand)
                    rate(last, slot)
                    attend(r, n, 1 - slot)

                fewer = n

        return jnp.where(mine, r, last), jnp.where(mine, 1 - slot, slot)

    table_ref[...] = before_ref[...]
    least_ref[...] = jnp.ones(least_ref.shape, jnp.float32)
    most_ref[...] = jnp.ones(most_ref.shape, jnp.float32)
    context_ref[...] = jnp.zeros(context_ref.shape, jnp.bfloat16)
    last, slot = lax.fori_loop(0, requests, one_request, (jnp.int32(-1), jnp.int32(0)))

    @pl.when(last >= 0)
    def _():
        rate(last, slot)

    in_range = (jnp.min(least_ref[...]) >= SUM_LEAST) & (jnp.max(most_ref[...]) <= SUM_MOST)
    again = jnp.logical_not(in_range) | (before_flag_ref[0] > 0)
    flag_ref[0] = again.astype(jnp.int32)
    if not spare:
        return
    for r in range(requests):
        again = again | ((count_ref[r] > 0) & (span_ref[requests + r] + 1 >= to_place))

    def exactly(r, carry):
        @pl.when(count_ref[r] > 0)
        def _():
            for copy in copies_of(r):
                copy.start()
            for copy in copies_of(r):
                copy.wait()
            load(r, slots, len(bases))
            attend_exactly(r, 0)
            rate(r, 0)

        return carry

    @pl.when(again)
    def _():
        arrivals[-1].start()
        arrivals[-1].wait()
        table_ref[...] = jnp.zeros(table_ref.shape, jnp.float32)
        lax.fori_loop(0, requests, exactly, 0)


def score(scalars, operands, arrived, weights, before, places, spare=False):
    base, queries, columns, ranks, _ = operands
    cands, width = base.shape[1], arrived[0].shape[2]
    slots = ranks.shape[1]
    devices = arrived[0].shape[0]
    bases = []
    for rows in arrived:
        bases.append(bases[-1] + arrived[len(bases) - 1].shape[1] // BLOCK if bases else 0)
    operands = [*operands, *arrived, *weights, before]
    return pl.pallas_call(
        functools.partial(
            score_kernel,
            bases=tuple(bases),
            from_place=places[0],
            to_place=places[1],
            spare=spare,
        ),
        in_specs=[whole(pltpu.SMEM)] * 4
        + [whole(pl.ANY)] * 3
        + [whole()] * 2
        + [whole(pl.ANY)] * len(arrived)
        + [whole() for _ in (*weights, before)],
        out_specs=[whole(), whole(pltpu.SMEM)],
        scratch_shapes=[
            pltpu.VMEM((slots, width), jnp.float32),
            pltpu.VMEM((HEADS, LANES, slots), jnp.bfloat16),
            pltpu.VMEM((HEADS // 2, 2 * slots, LANES), jnp.bfloat16),
            pltpu.VMEM((2, cands, width), jnp.bfloat16),
            pltpu.VMEM((ROWS_AT_ONCE, 1), jnp.float32),
            pltpu.VMEM((ROWS_AT_ONCE, 1), jnp.float32),
            pltpu.VMEM((LANES, devices), jnp.bfloat16),
            pltpu.VMEM(base.shape, base.dtype),
            pltpu.VMEM(queries.shape, queries.dtype),
            pltpu.VMEM(columns.shape, columns.dtype),
            pltpu.SemaphoreType.DMA((len(arrived),)),
            pltpu.SemaphoreType.DMA((3, ranks.shape[0])),
            *(pltpu.VMEM(rows.shape, rows.dtype) for rows in arrived),
        ],
        out_shape=[
            jax.ShapeDtypeStruct(before.shape, jnp.float32),
            jax.ShapeDtypeStruct((1,), jnp.int32),
        ],
        compiler_params=pltpu.CompilerParams(vmem_limit_bytes=VMEM_LIMIT),
        cost_estimate=pl.CostEstimate(
            flops=10_000_000_000, bytes_accessed=5_000_000, transcendentals=4_000_000
        ),
        name="score",
    )(*scalars, *operands)


def on_device(
    store_rows,
    cluster_logsize,
    cluster_home,
    cluster_ids,
    valid_count,
    candidates,
    cand_count,
    candidate_row,
    query_proj,
    key_proj,
    value_proj,
    out_proj,
    mlp_first,
    bias_first,
    mlp_second,
    bias_second,
    score_proj,
):
    axes = ("store", "scorer")
    devices = lax.axis_size(axes)
    scorers = lax.axis_size("scorer")
    requests, slots = cluster_ids.shape
    rows_dev, width = store_rows.shape
    cands = candidates.shape[1]
    per_pair = requests * slots // devices
    span_live = requests * cands // 2

    exchange = functools.partial(
        lax.all_to_all, axis_name=axes, split_axis=0, concat_axis=0, tiled=True
    )
    asked, ranks, span = ask(
        valid_count,
        cand_count,
        cluster_ids,
        cluster_home.reshape(-1, LANES),
        devices,
        per_pair,
        rows_dev,
    )
    asked_here = exchange(asked)
    in_blocks = lambda places: -(-places // BLOCK) * BLOCK
    early = in_blocks(per_pair // 2)
    cuts = (0, early, in_blocks(7 * per_pair // 8), in_blocks(per_pair + 1))
    lookup = (asked_here, store_rows, cluster_logsize.reshape(-1, LANES))
    early_here, most = serve(*lookup, asked_here, 0, [early], True)
    early_rows = exchange(early_here)
    queries, base, columns, score_cols = prep(
        candidates,
        query_proj,
        mlp_first,
        bias_first.reshape(1, -1),
        score_proj.reshape(1, -1),
        ranks,
        early_here,
    )
    last_rows = lax.cond(
        most[0] + 1 > cuts[2],
        lambda: exchange(serve(*lookup, score_cols, cuts[2], [cuts[3] - cuts[2]], False)[0]),
        lambda: jnp.zeros((devices, cuts[3] - cuts[2], width), jnp.bfloat16),
    )
    late_here, _ = serve(*lookup, last_rows, cuts[1], [cuts[2] - cuts[1]], False)
    weights = (
        key_proj.T,
        value_proj,
        out_proj,
        mlp_first,
        mlp_second,
        bias_second.reshape(1, -1),
        score_cols,
    )
    table = jnp.zeros((scorers * span_live // LANES, LANES), jnp.float32)
    scalars = (valid_count, cand_count, span)
    shared = (base, queries, columns, ranks, candidate_row)
    late_here, early_rows = lax.optimization_barrier((late_here, early_rows))
    late_rows = exchange(late_here)
    no_flag = jnp.zeros((1,), jnp.int32)
    arrived = (early_rows,)
    table, flag = score((*scalars, no_flag), shared, arrived, weights, table, cuts[0:2])
    arrived = (early_rows, late_rows, last_rows)
    table, _ = score((*scalars, flag), shared, arrived, weights, table, cuts[1:3], spare=True)
    parts = lax.all_to_all(
        table.reshape(scorers, span_live // LANES, LANES),
        "scorer",
        split_axis=0,
        concat_axis=0,
        tiled=True,
    )
    return jnp.sum(parts, axis=0).reshape(span_live)


def solution(mesh):
    rows = P(("store", "scorer"))
    in_specs = (
        P(("store", "scorer"), None),
        rows,
        P(),
        P(("store", "scorer"), None),
        rows,
        P(("store", "scorer"), None, None),
        rows,
        P(("store", "scorer"), None),
    ) + (P(),) * 9
    return jax.shard_map(
        on_device, mesh=mesh, in_specs=in_specs, out_specs=rows, check_vma=False
    )
```

```python
import functools
import math

import jax
import jax.numpy as jnp
from jax import lax
from jax.experimental import pallas as pl
from jax.experimental.pallas import tpu as pltpu
from jax.sharding import PartitionSpec as P

HEADS = 4
LANES = 128
BLOCK = 16
DEAD = -1e30
HIGH = 65536
OFFSET_PIECES = 3
ROWS_AT_ONCE = 64
SUM_LEAST = 2.0**-100
SUM_MOST = 2.0**100
VMEM_LIMIT = 40 * 1024 * 1024


def dot(a, b):
    return jnp.dot(a, b, preferred_element_type=jnp.float32)


def dot_nt(a, b):
    return lax.dot_general(a, b, (((1,), (1,)), ((), ())), preferred_element_type=jnp.float32)


def hot(mask):
    return jnp.where(mask, 1.0, 0.0).astype(jnp.bfloat16)


def iota(shape, axis):
    return lax.broadcasted_iota(jnp.int32, shape, axis)


def whole(memory_space=pltpu.VMEM):
    return pl.BlockSpec(memory_space=memory_space)


def look_up(table_t, index, pieces):
    highs = table_t.shape[1]
    count = index.shape[1]
    rows = dot(table_t, hot(iota((highs, count), 0) == (index >> 7)))
    mine = iota((LANES, count), 0) == (index & (LANES - 1))
    found = jnp.zeros((1, count), jnp.float32)
    for piece in range(pieces):
        part = rows[piece * LANES : (piece + 1) * LANES]
        found = found + float(256**piece) * jnp.sum(
            jnp.where(mine, part, 0.0), axis=0, keepdims=True
        )
    return found


def ask_kernel(
    valid_ref, count_ref, ids_ref, home_ref, asked_ref, rank_ref, span_ref, table_ref, *, rows_dev
):
    requests, slots = ids_ref.shape
    devices, per_pair = asked_ref.shape
    pieces = table_ref.shape[0] // LANES
    for piece in range(pieces):
        part = (home_ref[...] >> (8 * piece)) & 255
        table_ref[piece * LANES : (piece + 1) * LANES, :] = jnp.transpose(
            part.astype(jnp.float32)
        ).astype(jnp.bfloat16)
    table = table_ref[...]
    upto = hot(iota((slots, slots), 0) <= iota((slots, slots), 1))
    carry = jnp.zeros((devices, 1), jnp.float32)
    asked = jnp.zeros((devices, 2 * per_pair), jnp.float32)
    for r in range(requests):
        row = look_up(table, ids_ref[r : r + 1, :], pieces).astype(jnp.int32)
        dev = row // rows_dev
        local = row - dev * rows_dev
        live = iota((1, slots), 1) < jnp.where(count_ref[r] > 0, valid_ref[r], 0)
        dest = jnp.where((iota((devices, slots), 0) == dev) & live, 1.0, 0.0)
        running = dot(dest.astype(jnp.bfloat16), upto) + carry
        carry = running[:, slots - 1 : slots]
        rank_f = jnp.sum(dest * running, axis=0, keepdims=True) - 1.0
        rank = rank_f.astype(jnp.int32)
        at_rank = iota((per_pair, slots), 0) == rank
        local_f = local.astype(jnp.float32)
        high_f = (local >> 8).astype(jnp.float32)
        low_f = local_f - 256.0 * high_f
        values = jnp.concatenate(
            [jnp.where(at_rank, low_f, 0.0), jnp.where(at_rank, high_f, 0.0)], axis=0
        )
        asked = asked + dot_nt(dest.astype(jnp.bfloat16), values.astype(jnp.bfloat16))
        rank_ref[r : r + 1, :] = jnp.where(live, dev * LANES + rank, -1)
        span_ref[r] = jnp.min(jnp.where(live, rank_f, 1e9)).astype(jnp.int32)
        span_ref[requests + r] = jnp.max(rank_f).astype(jnp.int32)
    most = jnp.max(carry, axis=0, keepdims=True)
    asked = asked[:, :per_pair] + 256.0 * asked[:, per_pair:] + HIGH * most
    asked_ref[...] = asked.astype(jnp.int32)


def ask(valid_count, cand_count, cluster_ids, home_table, devices, per_pair, rows_dev):
    requests, slots = cluster_ids.shape
    highs = home_table.shape[0]
    pieces = -(-(highs * LANES - 1).bit_length() // 8)
    return pl.pallas_call(
        functools.partial(ask_kernel, rows_dev=rows_dev),
        in_specs=[whole(pltpu.SMEM), whole(pltpu.SMEM), whole(), whole()],
        out_specs=[whole(), whole(), whole(pltpu.SMEM)],
        out_shape=[
            jax.ShapeDtypeStruct((devices, per_pair), jnp.int32),
            jax.ShapeDtypeStruct((requests, slots), jnp.int32),
            jax.ShapeDtypeStruct((2 * requests,), jnp.int32),
        ],
        scratch_shapes=[pltpu.VMEM((pieces * LANES, highs), jnp.bfloat16)],
        compiler_params=pltpu.CompilerParams(vmem_limit_bytes=VMEM_LIMIT),
        cost_estimate=pl.CostEstimate(
            flops=4_000_000_000, bytes_accessed=1_000_000, transcendentals=0
        ),
        name="ask",
    )(valid_count, cand_count, cluster_ids, home_table)


def serve_kernel(asked_ref, store_ref, size_ref, after_ref, *refs, first, sized):
    del after_ref
    *out_refs, most_ref, column_ref = refs
    devices, per_pair = asked_ref.shape
    rows_dev, width = store_ref.shape
    places = max(out_ref.shape[1] for out_ref in out_refs)
    most_ref[0] = jnp.max((asked_ref[...] // HIGH).astype(jnp.float32)).astype(jnp.int32)
    asked = asked_ref[...] & (HIGH - 1)
    column_ref[...] = jnp.zeros(column_ref.shape, jnp.int32)
    column_ref[1 : per_pair + 1, :] = jnp.transpose(asked.astype(jnp.float32)).astype(jnp.int32)
    group = math.gcd(devices, 1 << (384 // places).bit_length() - 1)
    store = store_ref[...]
    lanes = iota((places, rows_dev), 1)
    if sized:
        size_t = jnp.transpose(size_ref[...].astype(jnp.float32)).astype(jnp.bfloat16)
    for start in range(0, devices, group):
        picks = []
        for d in range(start, start + group):
            column = column_ref[first : first + places, d : d + 1]
            picks.append(hot(column == lanes))
        found = dot(jnp.concatenate(picks, axis=0), store).reshape(group, places, width)
        if sized:
            asked_of = [asked[d : d + 1, :] for d in range(start, start + group)]
            sizes = look_up(size_t, jnp.concatenate(asked_of, axis=1), 1)
            rest = jnp.zeros((1, width - per_pair), jnp.float32)
            for g in range(group):
                mine = sizes[:, g * per_pair : (g + 1) * per_pair]
                mine = jnp.concatenate([mine, rest], axis=1)
                top = jnp.where(iota((places, width), 0) == 0, mine, found[g])
                out_refs[0][start + g] = top.astype(jnp.bfloat16)
        else:
            found = found.astype(jnp.bfloat16)
            for out_ref in out_refs:
                out_ref[start : start + group] = found[:, : out_ref.shape[1], :]


def serve(asked_here, store_rows, size_table, after, first, place_counts, sized):
    devices, per_pair = asked_here.shape
    rows_dev, width = store_rows.shape
    places = max(place_counts)
    column_rows = max(first + places, -(-(per_pair + 1) // BLOCK) * BLOCK)
    return pl.pallas_call(
        functools.partial(serve_kernel, first=first, sized=sized),
        in_specs=[whole(), whole(), whole(), whole(pl.ANY)],
        out_specs=[whole() for _ in place_counts] + [whole(pltpu.SMEM)],
        out_shape=[
            jax.ShapeDtypeStruct((devices, count, width), jnp.bfloat16) for count in place_counts
        ]
        + [jax.ShapeDtypeStruct((1,), jnp.int32)],
        scratch_shapes=[pltpu.VMEM((column_rows, devices), jnp.int32)],
        compiler_params=pltpu.CompilerParams(vmem_limit_bytes=VMEM_LIMIT),
        cost_estimate=pl.CostEstimate(
            flops=1_000_000, bytes_accessed=100_000, transcendentals=0
        ),
        name="serve",
    )(asked_here, store_rows, size_table, after)


def column_of(row):
    return jnp.transpose(jnp.broadcast_to(row, (LANES, row.shape[1])))


def row_of(ref, r, columns):
    part = ref[:, columns]
    mine = jnp.where(iota(part.shape, 0) == r, part.astype(jnp.float32), 0.0)
    return jnp.sum(mine, axis=0, keepdims=True).astype(jnp.int32)


def prep_kernel(cand_ref, query_ref, score_ref, rank_ref, after_ref, *out_refs):
    queries_ref, place_ref, score_cols_ref = out_refs
    devices = after_ref.shape[0]
    cands, width = cand_ref.shape[1:]
    size = width // HEADS
    lane = iota((cands, LANES), 1)
    score = jnp.broadcast_to(score_ref[...].astype(jnp.float32), (LANES, score_ref.shape[1]))
    score_cols_ref[...] = jnp.transpose(score).astype(jnp.bfloat16)

    def one_request(r, carry):
        queries = dot(cand_ref[r], query_ref[...])
        for h in range(HEADS):
            pair = queries[:, h // 2 * LANES : (h // 2 + 1) * LANES]
            own = lane // size == h % 2
            picks = jnp.where(lane % size < OFFSET_PIECES, 1.0, 0.0)
            queries_ref[r, h] = jnp.where(own, pair, picks).astype(jnp.bfloat16)
        spot = row_of(rank_ref, r, slice(None))
        at = (spot & (LANES - 1)) + 1
        place = (at // BLOCK) * (devices * BLOCK) + (spot // LANES) * BLOCK + at % BLOCK
        place_ref[r] = column_of(jnp.where(spot >= 0, place, -1))
        return carry

    lax.fori_loop(0, cand_ref.shape[0], one_request, 0)


def prep(candidates, query_proj, score_proj, ranks, after):
    requests, cands, width = candidates.shape
    return pl.pallas_call(
        prep_kernel,
        in_specs=[whole() for _ in range(4)] + [whole(pl.ANY)],
        out_specs=[whole() for _ in range(3)],
        out_shape=[
            jax.ShapeDtypeStruct((requests, HEADS, cands, LANES), jnp.bfloat16),
            jax.ShapeDtypeStruct((*ranks.shape, LANES), jnp.int32),
            jax.ShapeDtypeStruct((score_proj.shape[1], LANES), jnp.bfloat16),
        ],
        compiler_params=pltpu.CompilerParams(vmem_limit_bytes=VMEM_LIMIT),
        cost_estimate=pl.CostEstimate(
            flops=1_000_000, bytes_accessed=100_000, transcendentals=0
        ),
        name="prep",
    )(candidates, query_proj, score_proj, ranks, after)


def score_kernel(*refs, bases, from_place, to_place, spare):
    valid_ref, count_ref, span_ref, before_flag_ref = refs[:4]
    cand_all, queries_all, place_all, rank_ref, target_ref = refs[4:9]
    arrived_all = refs[9 : 9 + len(bases)]
    (
        key_ref,
        value_ref,
        out_proj_ref,
        first_ref,
        bias_first_ref,
        second_ref,
        bias_second_ref,
        score_ref,
        before_ref,
        table_ref,
        flag_ref,
        rows_ref,
        keys_ref,
        values_ref,
        context_ref,
        least_ref,
        most_ref,
        size_ref,
        cand_ref,
        queries_ref,
        place_ref,
        arrived_sems,
        request_sems,
        *arrived_refs,
    ) = refs[9 + len(bases) :]
    requests, slots = rank_ref.shape
    devices = arrived_refs[0].shape[0]
    cands, width = cand_ref.shape[1:]
    head_size = width // HEADS
    cand_part = math.gcd(cands, 256)
    highs = table_ref.shape[0]
    scale = math.sqrt(head_size)
    to_log2 = math.log2(math.e) / scale
    sizes_done = range(slots // 2, slots + 1, LANES)
    at_hand = len(bases) - 1 if spare else len(bases)
    fetched = ((place_all, place_ref), (queries_all, queries_ref), (cand_all, cand_ref))
    own_rows = [slice(h % 2 * head_size, (h % 2 + 1) * head_size) for h in range(HEADS)]
    other_rows = [slice((1 - h % 2) * head_size, (2 - h % 2) * head_size) for h in range(HEADS)]

    def is_mine(r):
        last_place = span_ref[requests + r] + 1
        return (count_ref[r] > 0) & (last_place >= from_place) & (last_place < to_place)

    def copies_of(r):
        return [
            pltpu.make_async_copy(source.at[r], target.at[r], request_sems.at[i, r])
            for i, (source, target) in enumerate(fetched)
        ]

    arrivals = [
        pltpu.make_async_copy(source, target, arrived_sems.at[i])
        for i, (source, target) in enumerate(zip(arrived_all, arrived_refs))
    ]
    for copy in arrivals[:at_hand]:
        copy.start()
    for r in range(requests):

        @pl.when(is_mine(r))
        def _():
            for copy in copies_of(r):
                copy.start()

    keys_ref[...] = jnp.zeros(keys_ref.shape, jnp.bfloat16)
    values_ref[...] = jnp.zeros(values_ref.shape, jnp.bfloat16)
    for copy in arrivals[:at_hand]:
        copy.wait()
    heads_of = arrived_refs[0][:, :BLOCK, :LANES].astype(jnp.float32)
    at_top = iota(heads_of.shape, 1) == 0
    sizes = jnp.sum(jnp.where(at_top, heads_of, 0.0), axis=1)
    size_ref[...] = jnp.transpose(sizes).astype(jnp.bfloat16)

    def select(r, n, arrived_ref, base):
        block_rows = devices * BLOCK
        blocks = arrived_ref.shape[1] // BLOCK
        at_once = min(2, blocks)
        low_block = jnp.clip((span_ref[r] + 1) // BLOCK - base, 0, blocks)
        high_block = jnp.clip((span_ref[requests + r] + 1) // BLOCK + 1 - base, 0, blocks)

        def step(i, carry):
            wanted = low_block + i * at_once
            j = jnp.minimum(wanted, blocks - at_once)
            place = place_ref[r, :n, :]
            rel = jnp.where(place >= (wanted + base) * block_rows, place, -1)
            rel = rel - (j + base) * block_rows
            lanes = iota((n, LANES), 1)
            found = []
            for b in range(at_once):
                start = pl.multiple_of((j + b) * BLOCK, BLOCK)
                block = arrived_ref[:, pl.ds(start, BLOCK), :].reshape(block_rows, width)
                firsts = range(b * block_rows, (b + 1) * block_rows, LANES)
                picks = [hot(rel == lanes + first) for first in firsts]
                found.append(dot(jnp.concatenate(picks, axis=1), block))
            rows_ref[:n, :] += sum(found)
            return carry

        lax.fori_loop(0, (high_block - low_block + at_once - 1) // at_once, step, 0)

    def load(r, n, blocks_at_hand):
        rows_ref[:n, :] = jnp.zeros((n, width), jnp.float32)
        for arrived_ref, base in list(zip(arrived_refs, bases))[:blocks_at_hand]:
            select(r, n, arrived_ref, base)
        spot = row_of(rank_ref, r, slice(0, n))
        size = look_up(size_ref[...], spot, 1)
        largest = jnp.max(jnp.where(spot >= 0, size, DEAD), axis=1, keepdims=True)
        left = jnp.where(spot >= 0, (size - largest) * scale, DEAD)
        pieces = jnp.zeros((head_size, n), jnp.float32)
        for row in range(OFFSET_PIECES):
            piece = left.astype(jnp.bfloat16).astype(jnp.float32)
            left = left - piece
            pieces = jnp.where(iota((head_size, n), 0) == row, piece, pieces)
        pieces = pieces.astype(jnp.bfloat16)
        rows = rows_ref[:n, :].astype(jnp.bfloat16)
        keys = dot_nt(key_ref[...], rows).astype(jnp.bfloat16)
        values = dot(rows, value_ref[...])
        own = iota((n, LANES), 1) // head_size
        for h in range(HEADS):
            keys_ref[h, own_rows[h], :n] = keys[h * head_size : (h + 1) * head_size]
            keys_ref[h, other_rows[h], :n] = pieces
            if n < slots:
                rest = (head_size, slots - n)
                dead = jnp.where(iota(rest, 0) == 0, DEAD, 0.0).astype(jnp.bfloat16)
                keys_ref[h, other_rows[h], n:] = dead
            pair = values[:, h // 2 * LANES : (h // 2 + 1) * LANES]
            first = h % 2 * n
            values_ref[h // 2, first : first + n, :] = jnp.where(own == h % 2, pair, 0.0).astype(
                jnp.bfloat16
            )

    def attend(r, n, slot):
        least = least_ref[...]
        most = most_ref[...]
        for pair in range(HEADS // 2):
            probs = []
            for h in (2 * pair, 2 * pair + 1):
                logits = dot(queries_ref[r, h], keys_ref[h, :, :n])
                of_head = []
                for first in range(0, cands, ROWS_AT_ONCE):
                    weights = jnp.exp2(logits[first : first + ROWS_AT_ONCE] * to_log2)
                    total = jnp.sum(weights, axis=1, keepdims=True)
                    least = jnp.minimum(least, total)
                    most = jnp.maximum(most, total)
                    of_head.append((weights * (1.0 / total)).astype(jnp.bfloat16))
                probs.append(jnp.concatenate(of_head, axis=0))
            context = dot(jnp.concatenate(probs, axis=1), values_ref[pair, : 2 * n, :])
            context_ref[slot, :, pair * LANES : (pair + 1) * LANES] = context.astype(jnp.bfloat16)
        least_ref[...] = least
        most_ref[...] = most

    def attend_exactly(r, slot):
        def part(c, carry):
            rows = pl.ds(pl.multiple_of(c * cand_part, cand_part), cand_part)
            for pair in range(HEADS // 2):
                probs = []
                for h in (2 * pair, 2 * pair + 1):
                    logits = dot(queries_ref[r, h, rows, :], keys_ref[h])
                    top = jnp.max(logits, axis=1, keepdims=True)
                    weights = jnp.exp2((logits - top) * to_log2)
                    total = jnp.sum(weights, axis=1, keepdims=True)
                    probs.append((weights * (1.0 / total)).astype(jnp.bfloat16))
                context = dot(jnp.concatenate(probs, axis=1), values_ref[pair])
                columns = slice(pair * LANES, (pair + 1) * LANES)
                context_ref[slot, rows, columns] = context.astype(jnp.bfloat16)
            return carry

        lax.fori_loop(0, cands // cand_part, part, 0)

    def rate(last, slot):
        r = jnp.maximum(last, 0)
        attended = dot(context_ref[slot], out_proj_ref[...]).astype(jnp.bfloat16)
        hidden = (
            dot(cand_ref[r], first_ref[:width, :])
            + dot(attended, first_ref[width:, :])
            + bias_first_ref[...]
        )
        hidden = jnp.maximum(hidden, 0.0).astype(jnp.bfloat16)
        hidden = dot(hidden, second_ref[...]) + bias_second_ref[...]
        hidden = jnp.maximum(hidden, 0.0).astype(jnp.bfloat16)
        scores = jnp.transpose(dot(hidden, score_ref[...]))[:1]
        target = row_of(target_ref, r, slice(None))
        counted = iota((1, cands), 1) < jnp.where(last >= 0, count_ref[r], 0)
        high_hot = hot((iota((highs, cands), 0) == (target >> 7)) & counted)
        at_low = iota((LANES, cands), 0) == (target & (LANES - 1))
        left = jnp.where(counted, scores, 0.0)
        pieces = []
        for _ in range(3):
            piece = left.astype(jnp.bfloat16).astype(jnp.float32)
            left = left - piece
            pieces.append(jnp.where(at_low, piece, 0.0).astype(jnp.bfloat16))
        found = dot_nt(high_hot, jnp.concatenate(pieces, axis=0))
        table_ref[...] += sum(found[:, i * LANES : (i + 1) * LANES] for i in range(3))

    def one_request(r, carry):
        last, slot = carry
        valid = valid_ref[r]
        mine = is_mine(r)

        @pl.when(mine)
        def _():
            for copy in copies_of(r):
                copy.wait()
            fewer = 0
            for n in sizes_done:

                @pl.when((valid > fewer) & (valid <= n))
                def _():
                    load(r, n, at_hand)
                    rate(last, slot)
                    attend(r, n, 1 - slot)

                fewer = n

        return jnp.where(mine, r, last), jnp.where(mine, 1 - slot, slot)

    table_ref[...] = before_ref[...]
    least_ref[...] = jnp.ones(least_ref.shape, jnp.float32)
    most_ref[...] = jnp.ones(most_ref.shape, jnp.float32)
    context_ref[...] = jnp.zeros(context_ref.shape, jnp.bfloat16)
    last, slot = lax.fori_loop(0, requests, one_request, (jnp.int32(-1), jnp.int32(0)))

    @pl.when(last >= 0)
    def _():
        rate(last, slot)

    in_range = (jnp.min(least_ref[...]) >= SUM_LEAST) & (jnp.max(most_ref[...]) <= SUM_MOST)
    again = jnp.logical_not(in_range) | (before_flag_ref[0] > 0)
    flag_ref[0] = again.astype(jnp.int32)
    if not spare:
        return
    for r in range(requests):
        again = again | ((count_ref[r] > 0) & (span_ref[requests + r] + 1 >= to_place))

    def exactly(r, carry):
        @pl.when(count_ref[r] > 0)
        def _():
            for copy in copies_of(r):
                copy.start()
            for copy in copies_of(r):
                copy.wait()
            load(r, slots, len(bases))
            attend_exactly(r, 0)
            rate(r, 0)

        return carry

    @pl.when(again)
    def _():
        arrivals[-1].start()
        arrivals[-1].wait()
        table_ref[...] = jnp.zeros(table_ref.shape, jnp.float32)
        lax.fori_loop(0, requests, exactly, 0)


def score(scalars, operands, arrived, weights, before, places, spare=False):
    candidates, queries, columns, ranks, _ = operands
    cands, width = candidates.shape[1:]
    slots = ranks.shape[1]
    devices = arrived[0].shape[0]
    bases = []
    for rows in arrived:
        bases.append(bases[-1] + arrived[len(bases) - 1].shape[1] // BLOCK if bases else 0)
    operands = [*operands, *arrived, *weights, before]
    return pl.pallas_call(
        functools.partial(
            score_kernel,
            bases=tuple(bases),
            from_place=places[0],
            to_place=places[1],
            spare=spare,
        ),
        in_specs=[whole(pltpu.SMEM)] * 4
        + [whole(pltpu.HBM)] * 3
        + [whole()] * 2
        + [whole(pltpu.HBM)] * len(arrived)
        + [whole() for _ in (*weights, before)],
        out_specs=[whole(), whole(pltpu.SMEM)],
        scratch_shapes=[
            pltpu.VMEM((slots, width), jnp.float32),
            pltpu.VMEM((HEADS, LANES, slots), jnp.bfloat16),
            pltpu.VMEM((HEADS // 2, 2 * slots, LANES), jnp.bfloat16),
            pltpu.VMEM((2, cands, width), jnp.bfloat16),
            pltpu.VMEM((ROWS_AT_ONCE, 1), jnp.float32),
            pltpu.VMEM((ROWS_AT_ONCE, 1), jnp.float32),
            pltpu.VMEM((LANES, devices), jnp.bfloat16),
            pltpu.VMEM(candidates.shape, candidates.dtype),
            pltpu.VMEM(queries.shape, queries.dtype),
            pltpu.VMEM(columns.shape, columns.dtype),
            pltpu.SemaphoreType.DMA((len(arrived),)),
            pltpu.SemaphoreType.DMA((3, ranks.shape[0])),
            *(pltpu.VMEM(rows.shape, rows.dtype) for rows in arrived),
        ],
        out_shape=[
            jax.ShapeDtypeStruct(before.shape, jnp.float32),
            jax.ShapeDtypeStruct((1,), jnp.int32),
        ],
        compiler_params=pltpu.CompilerParams(vmem_limit_bytes=VMEM_LIMIT),
        cost_estimate=pl.CostEstimate(
            flops=10_000_000_000, bytes_accessed=5_000_000, transcendentals=4_000_000
        ),
        name="score",
    )(*scalars, *operands)


def on_device(
    store_rows,
    cluster_logsize,
    cluster_home,
    cluster_ids,
    valid_count,
    candidates,
    cand_count,
    candidate_row,
    query_proj,
    key_proj,
    value_proj,
    out_proj,
    mlp_first,
    bias_first,
    mlp_second,
    bias_second,
    score_proj,
):
    axes = ("store", "scorer")
    devices = lax.axis_size(axes)
    scorers = lax.axis_size("scorer")
    requests, slots = cluster_ids.shape
    rows_dev, width = store_rows.shape
    cands = candidates.shape[1]
    per_pair = requests * slots // devices
    span_live = requests * cands // 2

    exchange = functools.partial(
        lax.all_to_all, axis_name=axes, split_axis=0, concat_axis=0, tiled=True
    )
    asked, ranks, span = ask(
        valid_count,
        cand_count,
        cluster_ids,
        cluster_home.reshape(-1, LANES),
        devices,
        per_pair,
        rows_dev,
    )
    asked_here = exchange(asked)
    in_blocks = lambda places: -(-places // BLOCK) * BLOCK
    early = in_blocks(per_pair // 2)
    cuts = (0, early, in_blocks(7 * per_pair // 8), in_blocks(per_pair + 1))
    lookup = (asked_here, store_rows, cluster_logsize.reshape(-1, LANES))
    early_here, most = serve(*lookup, asked_here, 0, [early], True)
    early_rows = exchange(early_here)
    queries, columns, score_cols = prep(
        candidates, query_proj, score_proj.reshape(1, -1), ranks, early_here
    )
    last_rows = lax.cond(
        most[0] + 1 > cuts[2],
        lambda: exchange(serve(*lookup, score_cols, cuts[2], [cuts[3] - cuts[2]], False)[0]),
        lambda: jnp.zeros((devices, cuts[3] - cuts[2], width), jnp.bfloat16),
    )
    late_here, _ = serve(*lookup, last_rows, cuts[1], [cuts[2] - cuts[1]], False)
    weights = (
        key_proj.T,
        value_proj,
        out_proj,
        mlp_first,
        bias_first.reshape(1, -1),
        mlp_second,
        bias_second.reshape(1, -1),
        score_cols,
    )
    table = jnp.zeros((scorers * span_live // LANES, LANES), jnp.float32)
    scalars = (valid_count, cand_count, span)
    shared = (candidates, queries, columns, ranks, candidate_row)
    late_here, early_rows = lax.optimization_barrier((late_here, early_rows))
    late_rows = exchange(late_here)
    no_flag = jnp.zeros((1,), jnp.int32)
    arrived = (early_rows,)
    table, flag = score((*scalars, no_flag), shared, arrived, weights, table, cuts[0:2])
    arrived = (early_rows, late_rows, last_rows)
    table, _ = score((*scalars, flag), shared, arrived, weights, table, cuts[1:3], spare=True)
    parts = lax.all_to_all(
        table.reshape(scorers, span_live // LANES, LANES),
        "scorer",
        split_axis=0,
        concat_axis=0,
        tiled=True,
    )
    return jnp.sum(parts, axis=0).reshape(span_live)


def solution(mesh):
    rows = P(("store", "scorer"))
    in_specs = (
        P(("store", "scorer"), None),
        rows,
        P(),
        P(("store", "scorer"), None),
        rows,
        P(("store", "scorer"), None, None),
        rows,
        P(("store", "scorer"), None),
    ) + (P(),) * 9
    return jax.shard_map(
        on_device, mesh=mesh, in_specs=in_specs, out_specs=rows, check_vma=False
    )
```

```python
import functools
import math

import jax
import jax.numpy as jnp
from jax import lax
from jax.experimental import pallas as pl
from jax.experimental.pallas import tpu as pltpu
from jax.sharding import PartitionSpec as P

HEADS = 4
LANES = 128
BLOCK = 16
DEAD = -1e30
HIGH = 65536
OFFSET_PIECES = 3
ROWS_AT_ONCE = 64
SUM_LEAST = 2.0**-100
SUM_MOST = 2.0**100
VMEM_LIMIT = 40 * 1024 * 1024


def dot(a, b):
    return jnp.dot(a, b, preferred_element_type=jnp.float32)


def dot_nt(a, b):
    return lax.dot_general(a, b, (((1,), (1,)), ((), ())), preferred_element_type=jnp.float32)


def hot(mask):
    return jnp.where(mask, 1.0, 0.0).astype(jnp.bfloat16)


def iota(shape, axis):
    return lax.broadcasted_iota(jnp.int32, shape, axis)


def whole(memory_space=pltpu.VMEM):
    return pl.BlockSpec(memory_space=memory_space)


def look_up(table_t, index, pieces):
    highs = table_t.shape[1]
    count = index.shape[1]
    rows = dot(table_t, hot(iota((highs, count), 0) == (index >> 7)))
    mine = iota((LANES, count), 0) == (index & (LANES - 1))
    found = jnp.zeros((1, count), jnp.float32)
    for piece in range(pieces):
        part = rows[piece * LANES : (piece + 1) * LANES]
        found = found + float(256**piece) * jnp.sum(
            jnp.where(mine, part, 0.0), axis=0, keepdims=True
        )
    return found


def ask_kernel(
    valid_ref, count_ref, ids_ref, home_ref, asked_ref, rank_ref, span_ref, table_ref, *, rows_dev
):
    requests, slots = ids_ref.shape
    devices, per_pair = asked_ref.shape
    pieces = table_ref.shape[0] // LANES
    for piece in range(pieces):
        part = (home_ref[...] >> (8 * piece)) & 255
        table_ref[piece * LANES : (piece + 1) * LANES, :] = jnp.transpose(
            part.astype(jnp.float32)
        ).astype(jnp.bfloat16)
    table = table_ref[...]
    upto = hot(iota((slots, slots), 0) <= iota((slots, slots), 1))
    carry = jnp.zeros((devices, 1), jnp.float32)
    asked = jnp.zeros((devices, 2 * per_pair), jnp.float32)
    for r in range(requests):
        row = look_up(table, ids_ref[r : r + 1, :], pieces).astype(jnp.int32)
        dev = row // rows_dev
        local = row - dev * rows_dev
        live = iota((1, slots), 1) < jnp.where(count_ref[r] > 0, valid_ref[r], 0)
        dest = jnp.where((iota((devices, slots), 0) == dev) & live, 1.0, 0.0)
        running = dot(dest.astype(jnp.bfloat16), upto) + carry
        carry = running[:, slots - 1 : slots]
        rank_f = jnp.sum(dest * running, axis=0, keepdims=True) - 1.0
        rank = rank_f.astype(jnp.int32)
        at_rank = iota((per_pair, slots), 0) == rank
        local_f = local.astype(jnp.float32)
        high_f = (local >> 8).astype(jnp.float32)
        low_f = local_f - 256.0 * high_f
        values = jnp.concatenate(
            [jnp.where(at_rank, low_f, 0.0), jnp.where(at_rank, high_f, 0.0)], axis=0
        )
        asked = asked + dot_nt(dest.astype(jnp.bfloat16), values.astype(jnp.bfloat16))
        rank_ref[r : r + 1, :] = jnp.where(live, dev * LANES + rank, -1)
        span_ref[r] = jnp.min(jnp.where(live, rank_f, 1e9)).astype(jnp.int32)
        span_ref[requests + r] = jnp.max(rank_f).astype(jnp.int32)
    most = jnp.max(carry, axis=0, keepdims=True)
    asked = asked[:, :per_pair] + 256.0 * asked[:, per_pair:] + HIGH * most
    asked_ref[...] = asked.astype(jnp.int32)


def ask(valid_count, cand_count, cluster_ids, home_table, devices, per_pair, rows_dev):
    requests, slots = cluster_ids.shape
    highs = home_table.shape[0]
    pieces = -(-(highs * LANES - 1).bit_length() // 8)
    return pl.pallas_call(
        functools.partial(ask_kernel, rows_dev=rows_dev),
        in_specs=[whole(pltpu.SMEM), whole(pltpu.SMEM), whole(), whole()],
        out_specs=[whole(), whole(), whole(pltpu.SMEM)],
        out_shape=[
            jax.ShapeDtypeStruct((devices, per_pair), jnp.int32),
            jax.ShapeDtypeStruct((requests, slots), jnp.int32),
            jax.ShapeDtypeStruct((2 * requests,), jnp.int32),
        ],
        scratch_shapes=[pltpu.VMEM((pieces * LANES, highs), jnp.bfloat16)],
        compiler_params=pltpu.CompilerParams(vmem_limit_bytes=VMEM_LIMIT),
        cost_estimate=pl.CostEstimate(
            flops=4_000_000_000, bytes_accessed=1_000_000, transcendentals=0
        ),
        name="ask",
    )(valid_count, cand_count, cluster_ids, home_table)


def serve_kernel(asked_ref, store_ref, size_ref, after_ref, *refs, first, sized):
    del after_ref
    *out_refs, most_ref, column_ref = refs
    devices, per_pair = asked_ref.shape
    rows_dev, width = store_ref.shape
    places = max(out_ref.shape[1] for out_ref in out_refs)
    most_ref[0] = jnp.max((asked_ref[...] // HIGH).astype(jnp.float32)).astype(jnp.int32)
    asked = asked_ref[...] & (HIGH - 1)
    column_ref[...] = jnp.zeros(column_ref.shape, jnp.int32)
    column_ref[1 : per_pair + 1, :] = jnp.transpose(asked.astype(jnp.float32)).astype(jnp.int32)
    group = math.gcd(devices, 1 << (384 // places).bit_length() - 1)
    store = store_ref[...]
    lanes = iota((places, rows_dev), 1)
    if sized:
        size_t = jnp.transpose(size_ref[...].astype(jnp.float32)).astype(jnp.bfloat16)
    for start in range(0, devices, group):
        picks = []
        for d in range(start, start + group):
            column = column_ref[first : first + places, d : d + 1]
            picks.append(hot(column == lanes))
        found = dot(jnp.concatenate(picks, axis=0), store).reshape(group, places, width)
        if sized:
            asked_of = [asked[d : d + 1, :] for d in range(start, start + group)]
            sizes = look_up(size_t, jnp.concatenate(asked_of, axis=1), 1)
            rest = jnp.zeros((1, width - per_pair), jnp.float32)
            for g in range(group):
                mine = sizes[:, g * per_pair : (g + 1) * per_pair]
                mine = jnp.concatenate([mine, rest], axis=1)
                top = jnp.where(iota((places, width), 0) == 0, mine, found[g])
                out_refs[0][start + g] = top.astype(jnp.bfloat16)
        else:
            found = found.astype(jnp.bfloat16)
            for out_ref in out_refs:
                out_ref[start : start + group] = found[:, : out_ref.shape[1], :]


def serve(asked_here, store_rows, size_table, after, first, place_counts, sized):
    devices, per_pair = asked_here.shape
    rows_dev, width = store_rows.shape
    places = max(place_counts)
    column_rows = max(first + places, -(-(per_pair + 1) // BLOCK) * BLOCK)
    return pl.pallas_call(
        functools.partial(serve_kernel, first=first, sized=sized),
        in_specs=[whole(), whole(), whole(), whole(pl.ANY)],
        out_specs=[whole() for _ in place_counts] + [whole(pltpu.SMEM)],
        out_shape=[
            jax.ShapeDtypeStruct((devices, count, width), jnp.bfloat16) for count in place_counts
        ]
        + [jax.ShapeDtypeStruct((1,), jnp.int32)],
        scratch_shapes=[pltpu.VMEM((column_rows, devices), jnp.int32)],
        compiler_params=pltpu.CompilerParams(vmem_limit_bytes=VMEM_LIMIT),
        cost_estimate=pl.CostEstimate(
            flops=2 * devices * places * rows_dev * width,
            bytes_accessed=2 * (rows_dev + devices * sum(place_counts)) * width,
            transcendentals=0,
        ),
        name="serve",
    )(asked_here, store_rows, size_table, after)


def column_of(row):
    return jnp.transpose(jnp.broadcast_to(row, (LANES, row.shape[1])))


def row_of(ref, r, columns):
    part = ref[:, columns]
    mine = jnp.where(iota(part.shape, 0) == r, part.astype(jnp.float32), 0.0)
    return jnp.sum(mine, axis=0, keepdims=True).astype(jnp.int32)


def prep_kernel(cand_ref, query_ref, score_ref, rank_ref, after_ref, *out_refs):
    queries_ref, place_ref, score_cols_ref = out_refs
    devices = after_ref.shape[0]
    cands, width = cand_ref.shape[1:]
    size = width // HEADS
    lane = iota((cands, LANES), 1)
    score = jnp.broadcast_to(score_ref[...].astype(jnp.float32), (LANES, score_ref.shape[1]))
    score_cols_ref[...] = jnp.transpose(score).astype(jnp.bfloat16)

    def one_request(r, carry):
        queries = dot(cand_ref[r], query_ref[...])
        for h in range(HEADS):
            pair = queries[:, h // 2 * LANES : (h // 2 + 1) * LANES]
            own = lane // size == h % 2
            picks = jnp.where(lane % size < OFFSET_PIECES, 1.0, 0.0)
            queries_ref[r, h] = jnp.where(own, pair, picks).astype(jnp.bfloat16)
        spot = row_of(rank_ref, r, slice(None))
        at = (spot & (LANES - 1)) + 1
        place = (at // BLOCK) * (devices * BLOCK) + (spot // LANES) * BLOCK + at % BLOCK
        place_ref[r] = column_of(jnp.where(spot >= 0, place, -1))
        return carry

    lax.fori_loop(0, cand_ref.shape[0], one_request, 0)


def prep(candidates, query_proj, score_proj, ranks, after):
    requests, cands, width = candidates.shape
    return pl.pallas_call(
        prep_kernel,
        in_specs=[whole() for _ in range(4)] + [whole(pl.ANY)],
        out_specs=[whole() for _ in range(3)],
        out_shape=[
            jax.ShapeDtypeStruct((requests, HEADS, cands, LANES), jnp.bfloat16),
            jax.ShapeDtypeStruct((*ranks.shape, LANES), jnp.int32),
            jax.ShapeDtypeStruct((score_proj.shape[1], LANES), jnp.bfloat16),
        ],
        compiler_params=pltpu.CompilerParams(vmem_limit_bytes=VMEM_LIMIT),
        cost_estimate=pl.CostEstimate(
            flops=2 * requests * cands * width * width,
            bytes_accessed=10 * requests * cands * width,
            transcendentals=0,
        ),
        name="prep",
    )(candidates, query_proj, score_proj, ranks, after)


def score_kernel(*refs, bases, from_place, to_place, spare):
    valid_ref, count_ref, span_ref, before_flag_ref = refs[:4]
    cand_all, queries_all, place_all, rank_ref, target_ref = refs[4:9]
    arrived_all = refs[9 : 9 + len(bases)]
    (
        key_ref,
        value_ref,
        out_proj_ref,
        first_ref,
        bias_first_ref,
        second_ref,
        bias_second_ref,
        score_ref,
        before_ref,
        table_ref,
        flag_ref,
        rows_ref,
        keys_ref,
        values_ref,
        context_ref,
        least_ref,
        most_ref,
        size_ref,
        cand_ref,
        queries_ref,
        place_ref,
        arrived_sems,
        request_sems,
        *arrived_refs,
    ) = refs[9 + len(bases) :]
    requests, slots = rank_ref.shape
    devices = arrived_refs[0].shape[0]
    cands, width = cand_ref.shape[1:]
    head_size = width // HEADS
    cand_part = math.gcd(cands, 256)
    highs = table_ref.shape[0]
    scale = math.sqrt(head_size)
    to_log2 = math.log2(math.e) / scale
    sizes_done = range(slots // 2, slots + 1, LANES)
    at_hand = len(bases) - 1 if spare else len(bases)
    fetched = ((place_all, place_ref), (queries_all, queries_ref), (cand_all, cand_ref))
    own_rows = [slice(h % 2 * head_size, (h % 2 + 1) * head_size) for h in range(HEADS)]
    other_rows = [slice((1 - h % 2) * head_size, (2 - h % 2) * head_size) for h in range(HEADS)]

    def is_mine(r):
        last_place = span_ref[requests + r] + 1
        return (count_ref[r] > 0) & (last_place >= from_place) & (last_place < to_place)

    def copies_of(r):
        return [
            pltpu.make_async_copy(source.at[r], target.at[r], request_sems.at[i, r])
            for i, (source, target) in enumerate(fetched)
        ]

    arrivals = [
        pltpu.make_async_copy(source, target, arrived_sems.at[i])
        for i, (source, target) in enumerate(zip(arrived_all, arrived_refs))
    ]
    for copy in arrivals[:at_hand]:
        copy.start()
    for r in range(requests):

        @pl.when(is_mine(r))
        def _():
            for copy in copies_of(r):
                copy.start()

    keys_ref[...] = jnp.zeros(keys_ref.shape, jnp.bfloat16)
    values_ref[...] = jnp.zeros(values_ref.shape, jnp.bfloat16)
    for copy in arrivals[:at_hand]:
        copy.wait()
    heads_of = arrived_refs[0][:, :BLOCK, :LANES].astype(jnp.float32)
    at_top = iota(heads_of.shape, 1) == 0
    sizes = jnp.sum(jnp.where(at_top, heads_of, 0.0), axis=1)
    size_ref[...] = jnp.transpose(sizes).astype(jnp.bfloat16)

    def select(r, n, arrived_ref, base):
        block_rows = devices * BLOCK
        blocks = arrived_ref.shape[1] // BLOCK
        at_once = min(2, blocks)
        low_block = jnp.clip((span_ref[r] + 1) // BLOCK - base, 0, blocks)
        high_block = jnp.clip((span_ref[requests + r] + 1) // BLOCK + 1 - base, 0, blocks)

        def step(i, carry):
            wanted = low_block + i * at_once
            j = jnp.minimum(wanted, blocks - at_once)
            place = place_ref[r, :n, :]
            rel = jnp.where(place >= (wanted + base) * block_rows, place, -1)
            rel = rel - (j + base) * block_rows
            lanes = iota((n, LANES), 1)
            found = []
            for b in range(at_once):
                start = pl.multiple_of((j + b) * BLOCK, BLOCK)
                block = arrived_ref[:, pl.ds(start, BLOCK), :].reshape(block_rows, width)
                firsts = range(b * block_rows, (b + 1) * block_rows, LANES)
                picks = [hot(rel == lanes + first) for first in firsts]
                found.append(dot(jnp.concatenate(picks, axis=1), block))
            rows_ref[:n, :] += sum(found)
            return carry

        lax.fori_loop(0, (high_block - low_block + at_once - 1) // at_once, step, 0)

    def load(r, n, blocks_at_hand):
        rows_ref[:n, :] = jnp.zeros((n, width), jnp.float32)
        for arrived_ref, base in list(zip(arrived_refs, bases))[:blocks_at_hand]:
            select(r, n, arrived_ref, base)
        spot = row_of(rank_ref, r, slice(0, n))
        size = look_up(size_ref[...], spot, 1)
        largest = jnp.max(jnp.where(spot >= 0, size, DEAD), axis=1, keepdims=True)
        left = jnp.where(spot >= 0, (size - largest) * scale, DEAD)
        pieces = jnp.zeros((head_size, n), jnp.float32)
        for row in range(OFFSET_PIECES):
            piece = left.astype(jnp.bfloat16).astype(jnp.float32)
            left = left - piece
            pieces = jnp.where(iota((head_size, n), 0) == row, piece, pieces)
        pieces = pieces.astype(jnp.bfloat16)
        rows = rows_ref[:n, :].astype(jnp.bfloat16)
        keys = dot_nt(key_ref[...], rows).astype(jnp.bfloat16)
        values = dot(rows, value_ref[...])
        own = iota((n, LANES), 1) // head_size
        for h in range(HEADS):
            keys_ref[h, own_rows[h], :n] = keys[h * head_size : (h + 1) * head_size]
            keys_ref[h, other_rows[h], :n] = pieces
            if n < slots:
                rest = (head_size, slots - n)
                dead = jnp.where(iota(rest, 0) == 0, DEAD, 0.0).astype(jnp.bfloat16)
                keys_ref[h, other_rows[h], n:] = dead
            pair = values[:, h // 2 * LANES : (h // 2 + 1) * LANES]
            first = h % 2 * n
            values_ref[h // 2, first : first + n, :] = jnp.where(own == h % 2, pair, 0.0).astype(
                jnp.bfloat16
            )

    def attend(r, n, slot):
        least = least_ref[...]
        most = most_ref[...]
        for pair in range(HEADS // 2):
            probs = []
            for h in (2 * pair, 2 * pair + 1):
                logits = dot(queries_ref[r, h], keys_ref[h, :, :n])
                of_head = []
                for first in range(0, cands, ROWS_AT_ONCE):
                    weights = jnp.exp2(logits[first : first + ROWS_AT_ONCE] * to_log2)
                    total = jnp.sum(weights, axis=1, keepdims=True)
                    least = jnp.minimum(least, total)
                    most = jnp.maximum(most, total)
                    of_head.append((weights * (1.0 / total)).astype(jnp.bfloat16))
                probs.append(jnp.concatenate(of_head, axis=0))
            context = dot(jnp.concatenate(probs, axis=1), values_ref[pair, : 2 * n, :])
            context_ref[slot, :, pair * LANES : (pair + 1) * LANES] = context.astype(jnp.bfloat16)
        least_ref[...] = least
        most_ref[...] = most

    def attend_exactly(r, slot):
        def part(c, carry):
            rows = pl.ds(pl.multiple_of(c * cand_part, cand_part), cand_part)
            for pair in range(HEADS // 2):
                probs = []
                for h in (2 * pair, 2 * pair + 1):
                    logits = dot(queries_ref[r, h, rows, :], keys_ref[h])
                    top = jnp.max(logits, axis=1, keepdims=True)
                    weights = jnp.exp2((logits - top) * to_log2)
                    total = jnp.sum(weights, axis=1, keepdims=True)
                    probs.append((weights * (1.0 / total)).astype(jnp.bfloat16))
                context = dot(jnp.concatenate(probs, axis=1), values_ref[pair])
                columns = slice(pair * LANES, (pair + 1) * LANES)
                context_ref[slot, rows, columns] = context.astype(jnp.bfloat16)
            return carry

        lax.fori_loop(0, cands // cand_part, part, 0)

    def rate(last, slot):
        r = jnp.maximum(last, 0)
        attended = dot(context_ref[slot], out_proj_ref[...]).astype(jnp.bfloat16)
        hidden = (
            dot(cand_ref[r], first_ref[:width, :])
            + dot(attended, first_ref[width:, :])
            + bias_first_ref[...]
        )
        hidden = jnp.maximum(hidden, 0.0).astype(jnp.bfloat16)
        hidden = dot(hidden, second_ref[...]) + bias_second_ref[...]
        hidden = jnp.maximum(hidden, 0.0).astype(jnp.bfloat16)
        scores = jnp.transpose(dot(hidden, score_ref[...]))[:1]
        target = row_of(target_ref, r, slice(None))
        counted = iota((1, cands), 1) < jnp.where(last >= 0, count_ref[r], 0)
        high_hot = hot((iota((highs, cands), 0) == (target >> 7)) & counted)
        at_low = iota((LANES, cands), 0) == (target & (LANES - 1))
        left = jnp.where(counted, scores, 0.0)
        pieces = []
        for _ in range(3):
            piece = left.astype(jnp.bfloat16).astype(jnp.float32)
            left = left - piece
            pieces.append(jnp.where(at_low, piece, 0.0).astype(jnp.bfloat16))
        found = dot_nt(high_hot, jnp.concatenate(pieces, axis=0))
        table_ref[...] += sum(found[:, i * LANES : (i + 1) * LANES] for i in range(3))

    def one_request(r, carry):
        last, slot = carry
        valid = valid_ref[r]
        mine = is_mine(r)

        @pl.when(mine)
        def _():
            for copy in copies_of(r):
                copy.wait()
            fewer = 0
            for n in sizes_done:

                @pl.when((valid > fewer) & (valid <= n))
                def _():
                    load(r, n, at_hand)
                    rate(last, slot)
                    attend(r, n, 1 - slot)

                fewer = n

        return jnp.where(mine, r, last), jnp.where(mine, 1 - slot, slot)

    table_ref[...] = before_ref[...]
    least_ref[...] = jnp.ones(least_ref.shape, jnp.float32)
    most_ref[...] = jnp.ones(most_ref.shape, jnp.float32)
    context_ref[...] = jnp.zeros(context_ref.shape, jnp.bfloat16)
    last, slot = lax.fori_loop(0, requests, one_request, (jnp.int32(-1), jnp.int32(0)))

    @pl.when(last >= 0)
    def _():
        rate(last, slot)

    in_range = (jnp.min(least_ref[...]) >= SUM_LEAST) & (jnp.max(most_ref[...]) <= SUM_MOST)
    again = jnp.logical_not(in_range) | (before_flag_ref[0] > 0)
    flag_ref[0] = again.astype(jnp.int32)
    if not spare:
        return
    for r in range(requests):
        again = again | ((count_ref[r] > 0) & (span_ref[requests + r] + 1 >= to_place))

    def exactly(r, carry):
        @pl.when(count_ref[r] > 0)
        def _():
            for copy in copies_of(r):
                copy.start()
            for copy in copies_of(r):
                copy.wait()
            load(r, slots, len(bases))
            attend_exactly(r, 0)
            rate(r, 0)

        return carry

    @pl.when(again)
    def _():
        arrivals[-1].start()
        arrivals[-1].wait()
        table_ref[...] = jnp.zeros(table_ref.shape, jnp.float32)
        lax.fori_loop(0, requests, exactly, 0)


def score(scalars, operands, arrived, weights, before, places, spare=False):
    candidates, queries, columns, ranks, _ = operands
    cands, width = candidates.shape[1:]
    slots = ranks.shape[1]
    devices = arrived[0].shape[0]
    bases = []
    for rows in arrived:
        bases.append(bases[-1] + arrived[len(bases) - 1].shape[1] // BLOCK if bases else 0)
    operands = [*operands, *arrived, *weights, before]
    return pl.pallas_call(
        functools.partial(
            score_kernel,
            bases=tuple(bases),
            from_place=places[0],
            to_place=places[1],
            spare=spare,
        ),
        in_specs=[whole(pltpu.SMEM)] * 4
        + [whole(pl.ANY)] * 3
        + [whole()] * 2
        + [whole(pl.ANY)] * len(arrived)
        + [whole() for _ in (*weights, before)],
        out_specs=[whole(), whole(pltpu.SMEM)],
        scratch_shapes=[
            pltpu.VMEM((slots, width), jnp.float32),
            pltpu.VMEM((HEADS, LANES, slots), jnp.bfloat16),
            pltpu.VMEM((HEADS // 2, 2 * slots, LANES), jnp.bfloat16),
            pltpu.VMEM((2, cands, width), jnp.bfloat16),
            pltpu.VMEM((ROWS_AT_ONCE, 1), jnp.float32),
            pltpu.VMEM((ROWS_AT_ONCE, 1), jnp.float32),
            pltpu.VMEM((LANES, devices), jnp.bfloat16),
            pltpu.VMEM(candidates.shape, candidates.dtype),
            pltpu.VMEM(queries.shape, queries.dtype),
            pltpu.VMEM(columns.shape, columns.dtype),
            pltpu.SemaphoreType.DMA((len(arrived),)),
            pltpu.SemaphoreType.DMA((3, ranks.shape[0])),
            *(pltpu.VMEM(rows.shape, rows.dtype) for rows in arrived),
        ],
        out_shape=[
            jax.ShapeDtypeStruct(before.shape, jnp.float32),
            jax.ShapeDtypeStruct((1,), jnp.int32),
        ],
        compiler_params=pltpu.CompilerParams(vmem_limit_bytes=VMEM_LIMIT),
        cost_estimate=pl.CostEstimate(
            flops=10_000_000_000, bytes_accessed=5_000_000, transcendentals=4_000_000
        ),
        name="score",
    )(*scalars, *operands)


def on_device(
    store_rows,
    cluster_logsize,
    cluster_home,
    cluster_ids,
    valid_count,
    candidates,
    cand_count,
    candidate_row,
    query_proj,
    key_proj,
    value_proj,
    out_proj,
    mlp_first,
    bias_first,
    mlp_second,
    bias_second,
    score_proj,
):
    axes = ("store", "scorer")
    devices = lax.axis_size(axes)
    scorers = lax.axis_size("scorer")
    requests, slots = cluster_ids.shape
    rows_dev, width = store_rows.shape
    cands = candidates.shape[1]
    per_pair = requests * slots // devices
    span_live = requests * cands // 2

    exchange = functools.partial(
        lax.all_to_all, axis_name=axes, split_axis=0, concat_axis=0, tiled=True
    )
    asked, ranks, span = ask(
        valid_count,
        cand_count,
        cluster_ids,
        cluster_home.reshape(-1, LANES),
        devices,
        per_pair,
        rows_dev,
    )
    asked_here = exchange(asked)
    in_blocks = lambda places: -(-places // BLOCK) * BLOCK
    early = in_blocks(per_pair // 2)
    cuts = (0, early, in_blocks(7 * per_pair // 8), in_blocks(per_pair + 1))
    lookup = (asked_here, store_rows, cluster_logsize.reshape(-1, LANES))
    early_here, most = serve(*lookup, asked_here, 0, [early], True)
    early_rows = exchange(early_here)
    queries, columns, score_cols = prep(
        candidates, query_proj, score_proj.reshape(1, -1), ranks, early_here
    )
    late_here, _ = serve(*lookup, score_cols, cuts[1], [cuts[2] - cuts[1]], False)
    weights = (
        key_proj.T,
        value_proj,
        out_proj,
        mlp_first,
        bias_first.reshape(1, -1),
        mlp_second,
        bias_second.reshape(1, -1),
        score_cols,
    )
    table = jnp.zeros((scorers * span_live // LANES, LANES), jnp.float32)
    scalars = (valid_count, cand_count, span)
    shared = (candidates, queries, columns, ranks, candidate_row)
    late_here, early_rows = lax.optimization_barrier((late_here, early_rows))
    late_rows = exchange(late_here)
    last_rows = lax.cond(
        most[0] + 1 > cuts[2],
        lambda: exchange(serve(*lookup, late_rows, cuts[2], [cuts[3] - cuts[2]], False)[0]),
        lambda: jnp.zeros((devices, cuts[3] - cuts[2], width), jnp.bfloat16),
    )
    no_flag = jnp.zeros((1,), jnp.int32)
    arrived = (early_rows,)
    table, flag = score((*scalars, no_flag), shared, arrived, weights, table, cuts[0:2])
    arrived = (early_rows, late_rows, last_rows)
    table, _ = score((*scalars, flag), shared, arrived, weights, table, cuts[1:3], spare=True)
    parts = lax.all_to_all(
        table.reshape(scorers, span_live // LANES, LANES),
        "scorer",
        split_axis=0,
        concat_axis=0,
        tiled=True,
    )
    return jnp.sum(parts, axis=0).reshape(span_live)


def solution(mesh):
    rows = P(("store", "scorer"))
    in_specs = (
        P(("store", "scorer"), None),
        rows,
        P(),
        P(("store", "scorer"), None),
        rows,
        P(("store", "scorer"), None, None),
        rows,
        P(("store", "scorer"), None),
    ) + (P(),) * 9
    return jax.shard_map(
        on_device, mesh=mesh, in_specs=in_specs, out_specs=rows, check_vma=False
    )
```
